128 devices in a mesh: grp: 4 (over y), inner: 32 (over z, x, core).
Axes of the slice: x: 4, y: 4, z: 4, core: 2. Of those that a mesh axis runs over, the one named last changes fastest.
Arguments:
- amplitude: float32 [1024, 16384], P(('grp', 'inner')), may hold values from -6 to 6
- integrals: float32 [16384, 128, 128], P(('grp', 'inner')), may hold values from -0.09375 to 0.09375
- tile_owner: int32 [16384, 1], P(('grp', 'inner')), may hold values from 0 to 127; in each aligned block of 128 rows (0 to 127, 128 to 255, ...) at most 2 rows name the same one
- tile_row: int32 [16384], P(('grp', 'inner')), may hold values from 0 to 3
- tile_col: int32 [16384], P(('grp', 'inner')), may hold values from 0 to 127
Outputs:
- ladder: float32 [1024, 16384], P(('grp', 'inner'))
The draws below stay inside these ranges and needn't reach their ends.
Inputs may be any that keep to these rules, and one draw needn't show every extreme that they name: `tile_owner`: among the 128 tiles of one device no owner is named more than 2 times, a bound that some block reaches.
All inputs are finite; a program needn't handle non-finite values.
Results may differ from the reference program's by a relative error of at most 0.0001.
Values sent between devices are 32-bit elements; how exact they have to be, the bound alone decides.
No kernel may reach another device: no remote copies, remote signals or barrier semaphores. Data moves between devices by JAX's collectives and lax.ppermute only.
A program may use at most 192 MiB of HBM per device.

```python
import math
import jax
import jax.numpy as jnp
import numpy as np
from jax import lax

TW = 128
M_DEV = 4
ROWS_DEV = 8
VT_DEV = 128
CAP = 2
KA = 128
PAIRS = 1024
NVT = 16384
N_INNER = 32
DEVICES = 128


def touch_ends(values, rng, low, high):
    shape = values.shape
    index_at = [jax.random.randint(jax.random.fold_in(rng, axis), (), 0, shape[axis]) for axis in range(len(shape))]
    values = values.at[tuple(index_at)].set(low)
    longest = shape.index(max(shape))
    index_at[longest] = (index_at[longest] + 1) % shape[longest]
    return values.at[tuple(index_at)].set(high)


def shard_levels(key, extent, shards, smallest, high):
    loudness, own = 1.0, jax.random.fold_in(key, 6)
    for position, shards_of in shards:
        steps = jnp.exp(jax.random.uniform(jax.random.fold_in(own, position), (shards_of,), jnp.float32, smallest / len(shards), high / len(shards)))
        loudness = loudness * jnp.repeat(steps, extent[position] // shards_of).reshape([-1 if axis == position else 1 for axis in range(len(extent))])
    return loudness


def routed_block(rng, own, number, rows, amount, top, bound, lean):
    ranking = jax.random.permutation(rng, amount)
    crowded, common = shares(amount, rows * top, bound, lean, True), shares(amount, rows * top, bound, lean, False)
    places = jnp.arange(amount)

    def named(sizes, turn):
        used = int((sizes > 0).sum())
        fixed = max(1, used // 4)
        passed = fixed + (places - fixed + turn * (used - fixed)) % max(1, amount - fixed)
        return jnp.zeros((amount,), jnp.int32).at[ranking[jnp.where(places < fixed, places, passed)]].set(jnp.asarray(sizes, jnp.int32))

    sizes = jnp.where(number % 4 == 0, named(crowded, number // 4), named(common, number - number // 4 - 1))
    mixed = jax.random.permutation(jax.random.fold_in(own, 3), amount)
    source_of, sink = mixed[0:amount // 2 * 2:2], mixed[1:amount // 2 * 2:2]
    slack = jnp.minimum(sizes[source_of] - 1, bound - sizes[sink]) // 2
    slack = jnp.where((source_of == ranking[0]) | (sink == ranking[0]) | (sizes[sink] == 0), 0, jnp.maximum(slack, 0))
    passed = jax.random.randint(jax.random.fold_in(own, 4), (amount // 2,), 0, 1 << 20) % (slack + 1)
    sizes = sizes.at[source_of].add(-passed).at[sink].add(passed)
    members = jnp.searchsorted(jnp.cumsum(sizes), jnp.arange(rows * top), side="right").astype(jnp.int32)
    grid = members.reshape(top, rows).T
    grid = grid[jax.random.permutation(jax.random.fold_in(own, 1), rows)]
    turn = jax.random.randint(jax.random.fold_in(own, 2), (rows, 1), 0, top)
    return jnp.take_along_axis(grid, (jnp.arange(top)[None, :] + turn) % top, axis=1)


def shares(count, total, limit, slope, full):
    weights = [(1 << 20) // math.isqrt(grade ** slope) + 1 for grade in range(1, count + 1)]
    largest = limit if full else min(limit, max(-(-total // count), total * weights[0] // sum(weights)))
    least = 1 if total - largest >= count - 1 else 0
    counts, rest = [largest] + [least] * (count - 1), total - largest - least * (count - 1)
    while rest > 0:
        movable = [i for i in range(1, count) if counts[i] < largest] or [i for i in range(1, count) if counts[i] < limit]
        mass, left = sum([weights[i] for i in movable]), rest
        for i in movable:
            more = min(limit - counts[i], max(1, left * weights[i] // mass), rest)
            counts[i] = counts[i] + more
            rest = rest - more
    return np.array(counts)


def bell_draw(rng, dims, scale, most, cuts=(), kind=jnp.bfloat16):
    gain = shard_levels(rng, dims, cuts, -0.22, 0.18) if cuts else 1.0
    entries = jax.random.normal(rng, dims, jnp.float32) * scale * gain
    return jnp.minimum(jnp.maximum(entries, -most), most).astype(kind)


def setup_inputs(seed: int = 0) -> dict:
    keys = jax.random.split(jax.random.key(seed), 6)
    amplitude = bell_draw(keys[0], (PAIRS, KA * TW), 1.0, 6.0, ((0, 128),), jnp.float32)
    integrals = bell_draw(keys[1], (NVT, TW, TW), (VT_DEV * TW // M_DEV) ** -0.5, 0.09375, ((0, 128),), jnp.float32)
    tile_owner_keys = jax.random.split(jax.random.fold_in(keys[2], 1), NVT // VT_DEV)
    tile_owner_turns = jax.random.permutation(jax.random.fold_in(keys[2], 3), NVT // VT_DEV)
    tile_owner = jax.vmap(lambda own, number: routed_block(jax.random.fold_in(keys[2], 2), own, number, VT_DEV, DEVICES, 1, CAP, 2))(tile_owner_keys, tile_owner_turns).reshape((NVT, 1))
    tile_row = touch_ends(jax.random.randint(keys[3], (NVT,), 0, M_DEV), jax.random.fold_in(keys[3], 1), 0, M_DEV - 1).astype(jnp.int32)
    tile_col = touch_ends(jax.random.randint(keys[4], (NVT,), 0, KA), jax.random.fold_in(keys[4], 1), 0, KA - 1).astype(jnp.int32)
    return {"amplitude": amplitude, "integrals": integrals, "tile_owner": tile_owner, "tile_row": tile_row, "tile_col": tile_col}


def reference(amplitude, integrals, tile_owner, tile_row, tile_col):
    tile_size = integrals.shape[1]
    slab_rows = ROWS_DEV * N_INNER
    owners = tile_owner[:, 0]

    def add_tile(tile_index, result):
        owner_now = owners[tile_index]
        group_index = owner_now // N_INNER
        inner_index = owner_now % N_INNER
        row_start = (group_index * slab_rows).astype(jnp.int32)
        col_left = ((inner_index * M_DEV + tile_row[tile_index]) * tile_size).astype(jnp.int32)
        col_right = (tile_col[tile_index] * tile_size).astype(jnp.int32)
        left_rows = lax.dynamic_slice(amplitude, (row_start, col_left), (slab_rows, tile_size))
        current = lax.dynamic_slice(result, (row_start, col_right), (slab_rows, tile_size))
        update = current + jnp.dot(left_rows, integrals[tile_index], precision=lax.Precision.HIGHEST, preferred_element_type=jnp.float32)
        return lax.dynamic_update_slice(result, update, (row_start, col_right))

    zeros_init = jnp.zeros(amplitude.shape, jnp.float32)
    return lax.fori_loop(0, integrals.shape[0], add_tile, zeros_init)
```

```python
import functools

import jax
import jax.numpy as jnp
from jax import lax
from jax.experimental import pallas as pl
from jax.experimental.pallas import tpu as pltpu
from jax.sharding import PartitionSpec as P

TILE = 128
STARTS = (0, 14, 27, 40)
OPEN = (0, 0, 0, 128)
VMEM = 50 * 1024 * 1024
AXES = ("grp", "inner")


def slow_part(amplitude, integrals, tile_owner, tile_row, tile_col):
    n_grp, n_inner = lax.axis_size("grp"), lax.axis_size("inner")
    devices = n_grp * n_inner
    count, size = integrals.shape[:2]
    blocks = amplitude.shape[1] // size
    per_dev = blocks // n_inner
    capacity = max(2, 2 * count // devices)
    owners = tile_owner[:, 0]
    order = jnp.arange(count, dtype=jnp.int32)
    same = (owners[:, None] == owners[None, :]) & (order[None, :] < order[:, None])
    slot = owners * capacity + jnp.sum(same.astype(jnp.int32), axis=1)
    position = (tile_row * blocks + tile_col).astype(jnp.float32)
    tiles = jnp.zeros((devices * capacity, size, size), jnp.float32).at[slot].set(integrals)
    place = jnp.zeros((devices * capacity,), jnp.float32).at[slot].set(position)
    tiles, place = (
        lax.all_to_all(tiles, AXES, split_axis=0, concat_axis=0, tiled=True),
        lax.all_to_all(place, AXES, split_axis=0, concat_axis=0, tiled=True),
    )
    dense = jnp.zeros((per_dev * blocks, size, size), jnp.float32).at[place.astype(jnp.int32)].add(tiles)
    dense = dense.reshape(per_dev, blocks, size, size).transpose(0, 2, 1, 3).reshape(per_dev * size, blocks * size)
    slab = lax.all_to_all(amplitude, "inner", split_axis=1, concat_axis=0, tiled=True)
    return lax.psum_scatter(
        jnp.dot(slab, dense, precision=lax.Precision.HIGHEST, preferred_element_type=jnp.float32),
        "inner",
        scatter_dimension=0,
        tiled=True,
    )


def pack_kernel(count, lists, first, index, tiles, *refs):
    outs, sems = refs[-len(lists) - 1 : -1], refs[-1]
    for at, which in enumerate(lists):

        def issue(k, _):
            pltpu.make_async_copy(tiles.at[index[which * first[1] + first[0] + k]], outs[at].at[k], sems.at[at]).start()
            return 0

        lax.fori_loop(0, count, issue, 0)
    for at in range(len(lists)):
        pltpu.make_async_copy(tiles.at[pl.ds(0, count)], outs[at], sems.at[at]).wait()


def pack(integrals, index, lists, start, count, total, after):
    any_spec = pl.BlockSpec(memory_space=pl.ANY)
    return pl.pallas_call(
        functools.partial(pack_kernel, count, lists, (start, total)),
        out_shape=[jax.ShapeDtypeStruct((count, TILE, TILE), jnp.float32)] * len(lists),
        in_specs=[pl.BlockSpec(memory_space=pltpu.SMEM), any_spec] + [any_spec] * len(after),
        out_specs=[any_spec] * len(lists),
        scratch_shapes=[pltpu.SemaphoreType.DMA((len(lists),))],
        cost_estimate=pl.CostEstimate(flops=0, bytes_accessed=2 * len(lists) * count * TILE * TILE * 4, transcendentals=0),
    )(index, integrals, *after)


def split(value):
    high = value.astype(jnp.bfloat16)
    return high, (value - high.astype(jnp.float32)).astype(jnp.bfloat16)


def ladder_kernel(count, lists, low, open_col, blocks, has_acc, *refs):
    refs = list(refs)
    code, where, amp = refs[:3]
    del refs[:3]
    acc_in = refs.pop(0) if has_acc else None
    tiles = refs[:lists]
    del refs[:lists]
    acc_out = refs.pop(0) if open_col < blocks else None
    parts = [refs.pop(0) for _ in range(8)] if open_col > low else []
    amp_v, acc_v, tile_v, amp_sem, acc_sem, tile_sem, out_sem = refs

    z, x = where[0], where[1]
    for sx in range(4):
        for sz in range(4):
            source = lax.rem(z + sz, 4) * 4 + lax.rem(x + sx, 4)
            pltpu.make_async_copy(amp.at[source], amp_v.at[sx * 4 + sz], amp_sem).start()
    if has_acc:
        acc_copy = pltpu.make_async_copy(acc_in, acc_v, acc_sem)
        acc_copy.start()
    copies = [pltpu.make_async_copy(tiles[k], tile_v.at[k], tile_sem.at[k]) for k in range(lists)]
    for copy in copies:
        copy.start()
    if has_acc:
        acc_copy.wait()
    else:
        acc_v[...] = jnp.zeros_like(acc_v)
    pltpu.make_async_copy(amp, amp_v, amp_sem).wait()

    for k in range(lists):
        copies[k].wait()

        def one(j, _):
            place = code[k * count + j]

            @pl.when(place >= 0)
            def _():
                row = pl.multiple_of((place // blocks) * TILE, TILE)
                col = pl.multiple_of((lax.rem(place, blocks) - low) * TILE, TILE)
                a_hi, a_lo = split(amp_v[:, :, pl.ds(row, TILE)].reshape(16 * 8, TILE))
                t_hi, t_lo = split(tile_v[k, j])
                left = jnp.concatenate([a_hi, a_lo], axis=1)
                right = jnp.concatenate([t_hi, t_lo], axis=1)
                both = jnp.dot(left, jnp.concatenate([right, right], axis=0), preferred_element_type=jnp.float32)
                term = both[:, :TILE] + both[:, TILE:]
                acc_v[:, :, :, pl.ds(col, TILE)] += term.reshape(4, 4, 8, TILE)

            return 0

        lax.fori_loop(0, count, one, 0)

    done = []
    if acc_out is not None:
        done.append(pltpu.make_async_copy(acc_v.at[:, :, :, pl.ds((open_col - low) * TILE, (blocks - open_col) * TILE)], acc_out, out_sem.at[8]))
    if parts:
        half = (open_col - low) * TILE // 2
        for s in range(4):
            done.append(pltpu.make_async_copy(acc_v.at[s, :, :, pl.ds(0, half)], parts[s], out_sem.at[s]))
            done.append(pltpu.make_async_copy(acc_v.at[:, s, :, pl.ds(half, half)], parts[4 + s], out_sem.at[4 + s]))
    for copy in done:
        copy.start()
    for copy in done:
        copy.wait()


def ladder(code, where, amp, acc, tiles, low, open_col, blocks):
    lists, count = len(tiles), tiles[0].shape[0]
    any_spec, smem = pl.BlockSpec(memory_space=pl.ANY), pl.BlockSpec(memory_space=pltpu.SMEM)
    shapes = []
    if open_col < blocks:
        shapes.append(jax.ShapeDtypeStruct((4, 4, 8, (blocks - open_col) * TILE), jnp.float32))
    if open_col > low:
        shapes += [jax.ShapeDtypeStruct((4, 8, (open_col - low) * TILE // 2), jnp.float32)] * 8
    given = [code, where, amp] + ([] if acc is None else [acc]) + list(tiles)
    outs = pl.pallas_call(
        functools.partial(ladder_kernel, count, lists, low, open_col, blocks, acc is not None),
        out_shape=shapes,
        in_specs=[smem, smem] + [any_spec] * (len(given) - 2),
        out_specs=[any_spec] * len(shapes),
        scratch_shapes=[
            pltpu.VMEM((16, 8, blocks * TILE), jnp.float32),
            pltpu.VMEM((4, 4, 8, (blocks - low) * TILE), jnp.float32),
            pltpu.VMEM((lists, count, TILE, TILE), jnp.float32),
            pltpu.SemaphoreType.DMA,
            pltpu.SemaphoreType.DMA,
            pltpu.SemaphoreType.DMA((lists,)),
            pltpu.SemaphoreType.DMA((9,)),
        ],
        compiler_params=pltpu.CompilerParams(vmem_limit_bytes=VMEM),
        cost_estimate=pl.CostEstimate(flops=lists * count * 2 * 128**3 * 4, bytes_accessed=24 * 2**20, transcendentals=0),
    )(*given)
    outs = list(outs)
    acc = outs.pop(0) if open_col < blocks else None
    return acc, outs


def per_device(amplitude, integrals, tile_owner, tile_row, tile_col):
    n_grp, n_inner = lax.axis_size("grp"), lax.axis_size("inner")
    devices = n_grp * n_inner
    rows, width = amplitude.shape
    count = integrals.shape[0]
    blocks = width // TILE
    per_dev = blocks // n_inner
    total = STARTS[-1]
    chunks = len(STARTS) - 1
    grp, inner = lax.axis_index("grp"), lax.axis_index("inner")
    z, x, core = inner // 8, (inner // 2) % 4, inner % 2

    def at(z, x, core):
        return (z % 4) * 8 + (x % 4) * 2 + core

    every = [(a, b, c) for a in range(4) for b in range(4) for c in range(2)]
    along_x = {s: [(at(a, b, c), at(a, b + s, c)) for a, b, c in every] for s in (1, 2, 3)}
    along_z = {s: [(at(a, b, c), at(a + s, b, c)) for a, b, c in every] for s in (1, 2, 3)}
    along_y = {s: [(i, (i + s) % n_grp) for i in range(n_grp)] for s in (1, 2, 3)}
    across = [(i, i ^ 1) for i in range(n_inner)]
    same_core = [[at(a, b, c) for a in range(4) for b in range(4)] for c in range(2)]

    amp = lax.all_gather(amplitude, "inner", axis=0, axis_index_groups=same_core)

    owners = tile_owner[:, 0]
    slab = owners // n_inner
    step = (slab - grp + n_grp) % n_grp
    order = jnp.arange(count, dtype=jnp.int32)
    key = tile_col * count + order
    ahead = (slab[:, None] == slab[None, :]) & (key[None, :] < key[:, None])
    rank = jnp.sum(ahead.astype(jnp.int32), axis=1)
    limit = jnp.full((count,), total, jnp.int32)
    for c in range(chunks - 1, 0, -1):
        limit = jnp.where(tile_col < OPEN[c], STARTS[c], limit)
    fits = rank < limit
    code = ((owners % n_inner) * per_dev + tile_row) * blocks + tile_col
    slots = jnp.arange(n_grp * total, dtype=jnp.int32)[:, None]
    mine = jnp.where(fits, step * total + rank, -1)[None, :] == slots
    index = jnp.sum(jnp.where(mine, order[None, :], 0), axis=1)
    theirs = jnp.where(fits, slab * total + rank, -1)[None, :] == slots
    codes = jnp.sum(jnp.where(theirs, code[None, :] + 1, 0), axis=1) - 1
    left_over = jnp.sum((~fits).astype(jnp.int32))

    got = []
    before_a, before_b = (), ()
    for c in range(chunks):
        lo, n = STARTS[c], STARTS[c + 1] - STARTS[c]
        p1, p3 = pack(integrals, index, (1, 3), lo, n, total, before_a)
        p2, p0 = pack(integrals, index, (2, 0), lo, n, total, before_b)
        r1, r3 = lax.ppermute(p1, "grp", along_y[1]), lax.ppermute(p3, "grp", along_y[3])
        r2 = lax.ppermute(p2, "grp", along_y[2])
        before_a, before_b = (r1, r3), (r2,)
        got.append((p0, r1, r2, r3))
        if c == 0:
            gate = p2
    codes, _ = lax.optimization_barrier((codes, gate))
    note = jnp.concatenate(
        [
            jnp.broadcast_to(codes.reshape(n_grp, 1, total), (n_grp, n_inner, total)),
            jnp.broadcast_to(left_over, (n_grp, n_inner, 1)),
        ],
        axis=2,
    ).astype(jnp.float32)
    note = lax.all_to_all(note.reshape(devices, total + 1), AXES, split_axis=0, concat_axis=0, tiled=True)
    overflow = jnp.sum(note[:, total]) > 0.5
    note = note[:, :total].reshape(n_grp, n_inner // 2, 2, total)
    note = lax.dynamic_index_in_dim(note, inner // 2, axis=1, keepdims=False)
    note = jnp.stack([lax.dynamic_index_in_dim(note, (grp - s + n_grp) % n_grp, axis=0, keepdims=False) for s in range(4)])
    note = jnp.stack([lax.dynamic_index_in_dim(note, core, axis=1, keepdims=False), lax.dynamic_index_in_dim(note, 1 - core, axis=1, keepdims=False)])
    note = note.astype(jnp.int32)
    where = jnp.stack([z, x]).astype(jnp.int32)

    acc, pieces = None, []
    for c in range(chunks):
        own = got[c]
        other = [lax.ppermute(t, "inner", across) for t in own]
        code_c = note[:, :, STARTS[c] : STARTS[c + 1]].reshape(-1)
        acc, parts = ladder(code_c, where, amp, acc, [*own, *other], OPEN[c], OPEN[c + 1], blocks)
        if parts:
            one, two = parts[:4], parts[4:]
            r1 = [lax.ppermute(one[s], "inner", along_x[s]) for s in (1, 3, 2)]
            r2 = [lax.ppermute(two[s], "inner", along_z[s]) for s in (1, 3, 2)]
            s1 = [one[0][q] + r1[0][q] + r1[1][q] + r1[2][q] for q in range(4)]
            s2 = [two[0][q] + r2[0][q] + r2[1][q] + r2[2][q] for q in range(4)]
            f1 = [lax.ppermute(s1[s], "inner", along_z[s]) for s in (1, 3, 2)]
            f2 = [lax.ppermute(s2[s], "inner", along_x[s]) for s in (1, 3, 2)]
            pieces += [s1[0] + f1[0] + f1[1] + f1[2], s2[0] + f2[0] + f2[1] + f2[2]]
    out = jnp.concatenate(pieces, axis=1)

    def with_rest(out):
        rest = jnp.where(fits[:, None, None], 0.0, integrals)
        return out + slow_part(amplitude, rest, tile_owner, tile_row, tile_col)

    return lax.cond(overflow, with_rest, lambda out: out, out)


def solution(mesh):
    placed = (P(AXES, None), P(AXES, None, None), P(AXES, None), P(AXES), P(AXES))
    return jax.shard_map(per_device, mesh=mesh, in_specs=placed, out_specs=P(AXES, None), check_vma=False)
```

```python
import functools

import jax
import jax.numpy as jnp
from jax import lax
from jax.experimental import pallas as pl
from jax.experimental.pallas import tpu as pltpu
from jax.sharding import PartitionSpec as P

TILE = 128
SLOTS = 40
FIRST = 30
VMEM = 60 * 1024 * 1024
AXES = ("grp", "inner")


def slow_part(amplitude, integrals, tile_owner, tile_row, tile_col):
    n_grp, n_inner = lax.axis_size("grp"), lax.axis_size("inner")
    devices = n_grp * n_inner
    count, size = integrals.shape[:2]
    blocks = amplitude.shape[1] // size
    per_dev = blocks // n_inner
    capacity = max(2, 2 * count // devices)
    owners = tile_owner[:, 0]
    order = jnp.arange(count, dtype=jnp.int32)
    same = (owners[:, None] == owners[None, :]) & (order[None, :] < order[:, None])
    slot = owners * capacity + jnp.sum(same.astype(jnp.int32), axis=1)
    position = (tile_row * blocks + tile_col).astype(jnp.float32)
    tiles = jnp.zeros((devices * capacity, size, size), jnp.float32).at[slot].set(integrals)
    place = jnp.zeros((devices * capacity,), jnp.float32).at[slot].set(position)
    tiles, place = (
        lax.all_to_all(tiles, AXES, split_axis=0, concat_axis=0, tiled=True),
        lax.all_to_all(place, AXES, split_axis=0, concat_axis=0, tiled=True),
    )
    dense = jnp.zeros((per_dev * blocks, size, size), jnp.float32).at[place.astype(jnp.int32)].add(tiles)
    dense = dense.reshape(per_dev, blocks, size, size).transpose(0, 2, 1, 3).reshape(per_dev * size, blocks * size)
    slab = lax.all_to_all(amplitude, "inner", split_axis=1, concat_axis=0, tiled=True)
    return lax.psum_scatter(
        jnp.dot(slab, dense, precision=lax.Precision.HIGHEST, preferred_element_type=jnp.float32),
        "inner",
        scatter_dimension=0,
        tiled=True,
    )


def pack_kernel(spans, total, index, tiles, *refs):
    outs, sems = refs[: len(spans)], refs[-1]
    for at, (which, lo, hi) in enumerate(spans):

        def issue(k, _):
            pltpu.make_async_copy(tiles.at[index[which * total + lo + k]], outs[at].at[k], sems.at[at]).start()
            return 0

        lax.fori_loop(0, hi - lo, issue, 0)
    for at, (_, lo, hi) in enumerate(spans):
        pltpu.make_async_copy(tiles.at[pl.ds(0, hi - lo)], outs[at], sems.at[at]).wait()


def pack(integrals, index, spans, total):
    return pl.pallas_call(
        functools.partial(pack_kernel, spans, total),
        out_shape=[jax.ShapeDtypeStruct((hi - lo, TILE, TILE), jnp.float32) for _, lo, hi in spans],
        in_specs=[pl.BlockSpec(memory_space=pltpu.SMEM), pl.BlockSpec(memory_space=pl.ANY)],
        out_specs=[pl.BlockSpec(memory_space=pltpu.VMEM)] * len(spans),
        scratch_shapes=[pltpu.SemaphoreType.DMA((len(spans),))],
        compiler_params=pltpu.CompilerParams(vmem_limit_bytes=VMEM),
        cost_estimate=pl.CostEstimate(flops=0, bytes_accessed=1000, transcendentals=0),
    )(index, integrals)


def add_kernel(one, two, out):
    out[...] = one[...] + two[...]


def add(one, two):
    return pl.pallas_call(add_kernel, out_shape=jax.ShapeDtypeStruct(one.shape, one.dtype))(one, two)


def gate_kernel(*refs):
    pass


def gate(value, *after):
    any_spec = pl.BlockSpec(memory_space=pl.ANY)
    return pl.pallas_call(
        gate_kernel,
        out_shape=jax.ShapeDtypeStruct(value.shape, value.dtype),
        in_specs=[any_spec] * (1 + len(after)),
        out_specs=any_spec,
        input_output_aliases={0: 0},
    )(value, *after)


def split(value):
    high = value.astype(jnp.bfloat16)
    return high, (value - high.astype(jnp.float32)).astype(jnp.bfloat16)


def ladder_kernel(counts, blocks, has_acc, last, *refs):
    refs, lists = list(refs), len(counts)
    code, where, amp = refs[:3]
    del refs[:3]
    acc_in = refs.pop(0) if has_acc else None
    tiles = refs[:lists]
    del refs[:lists]
    acc_out = None if last else refs.pop(0)
    parts = [refs.pop(0) for _ in range(8)] if last else []
    tile_v = refs[:lists]
    amp_v, acc_v, amp_sem, acc_sem, tile_sem, out_sem = refs[lists:]

    z, x = where[0], where[1]
    for sx in range(4):
        for sz in range(4):
            source = lax.rem(z + sz, 4) * 4 + lax.rem(x + sx, 4)
            pltpu.make_async_copy(amp.at[source], amp_v.at[sx * 4 + sz], amp_sem).start()
    if has_acc:
        acc_copy = pltpu.make_async_copy(acc_in, acc_v, acc_sem)
        acc_copy.start()
    copies = [pltpu.make_async_copy(tiles[k], tile_v[k], tile_sem.at[k]) for k in range(lists)]
    for copy in copies:
        copy.start()
    if has_acc:
        acc_copy.wait()
    else:
        acc_v[...] = jnp.zeros_like(acc_v)
    pltpu.make_async_copy(amp, amp_v, amp_sem).wait()

    for k in range(lists):
        copies[k].wait()
        base = sum(counts[:k])

        def pair(j, _):
            places = [code[base + 2 * j], code[base + 2 * j + 1]]

            @pl.when(jnp.maximum(*places) >= 0)
            def _():
                terms = []
                for half, place in enumerate(places):
                    held = jnp.maximum(place, 0)
                    row = pl.multiple_of((held // blocks) * TILE, TILE)
                    col = pl.multiple_of(lax.rem(held, blocks) * TILE, TILE)
                    a_hi, a_lo = split(amp_v[:, :, pl.ds(row, TILE)].reshape(16 * 8, TILE))
                    t_hi, t_lo = split(jnp.where(place >= 0, tile_v[k][2 * j + half], 0.0))
                    left = jnp.concatenate([a_hi, a_lo], axis=1)
                    right = jnp.concatenate([t_hi, t_lo], axis=1)
                    both = jnp.dot(left, jnp.concatenate([right, right], axis=0), preferred_element_type=jnp.float32)
                    terms.append((col, (both[:, :TILE] + both[:, TILE:]).reshape(4, 4, 8, TILE)))
                for col, term in terms:
                    acc_v[:, :, :, pl.ds(col, TILE)] += term

            return 0

        lax.fori_loop(0, counts[k] // 2, pair, 0)

    if last:
        done, half = [], blocks * TILE // 2
        for s in range(4):
            done.append(pltpu.make_async_copy(acc_v.at[s, :, :, pl.ds(0, half)], parts[s], out_sem.at[s]))
            done.append(pltpu.make_async_copy(acc_v.at[:, s, :, pl.ds(half, half)], parts[4 + s], out_sem.at[4 + s]))
    else:
        done = [pltpu.make_async_copy(acc_v, acc_out, out_sem.at[0])]
    for copy in done:
        copy.start()
    for copy in done:
        copy.wait()


def ladder(code, where, amp, acc, tiles, last, blocks, guess):
    counts = tuple(t.shape[0] for t in tiles)
    any_spec, smem = pl.BlockSpec(memory_space=pl.ANY), pl.BlockSpec(memory_space=pltpu.SMEM)
    if last:
        shapes = [jax.ShapeDtypeStruct((4, 8, blocks * TILE // 2), jnp.float32)] * 8
    else:
        shapes = [jax.ShapeDtypeStruct((4, 4, 8, blocks * TILE), jnp.float32)]
    given = [code, where, amp] + ([] if acc is None else [acc]) + list(tiles)
    return pl.pallas_call(
        functools.partial(ladder_kernel, counts, blocks, acc is not None, last),
        out_shape=shapes,
        in_specs=[smem, smem] + [any_spec] * (len(given) - 2),
        out_specs=[any_spec] * len(shapes),
        scratch_shapes=[
            *[pltpu.VMEM((n, TILE, TILE), jnp.float32) for n in counts],
            pltpu.VMEM((16, 8, blocks * TILE), jnp.float32),
            pltpu.VMEM((4, 4, 8, blocks * TILE), jnp.float32),
            pltpu.SemaphoreType.DMA,
            pltpu.SemaphoreType.DMA,
            pltpu.SemaphoreType.DMA((len(tiles),)),
            pltpu.SemaphoreType.DMA((9,)),
        ],
        compiler_params=pltpu.CompilerParams(vmem_limit_bytes=VMEM),
        cost_estimate=pl.CostEstimate(flops=0, bytes_accessed=guess, transcendentals=0),
    )(*given)


def per_device(amplitude, integrals, tile_owner, tile_row, tile_col):
    n_grp, n_inner = lax.axis_size("grp"), lax.axis_size("inner")
    devices = n_grp * n_inner
    rows, width = amplitude.shape
    count = integrals.shape[0]
    blocks = width // TILE
    per_dev = blocks // n_inner
    total = SLOTS
    grp, inner = lax.axis_index("grp"), lax.axis_index("inner")
    z, x, core = inner // 8, (inner // 2) % 4, inner % 2

    def at(z, x, core):
        return (z % 4) * 8 + (x % 4) * 2 + core

    every = [(a, b, c) for a in range(4) for b in range(4) for c in range(2)]
    along_x = {s: [(at(a, b, c), at(a, b + s, c)) for a, b, c in every] for s in (1, 2, 3)}
    along_z = {s: [(at(a, b, c), at(a + s, b, c)) for a, b, c in every] for s in (1, 2, 3)}
    along_y = {s: [(i, (i + s) % n_grp) for i in range(n_grp)] for s in (1, 2, 3)}
    across = [(i, i ^ 1) for i in range(n_inner)]
    same_core = [[at(a, b, c) for a in range(4) for b in range(4)] for c in range(2)]

    amp = lax.all_gather(amplitude, "inner", axis=0, axis_index_groups=same_core)

    owners = tile_owner[:, 0]
    slab = owners // n_inner
    step = (slab - grp + n_grp) % n_grp
    order = jnp.arange(count, dtype=jnp.int32)
    key = tile_col * count + order
    ahead = (slab[:, None] == slab[None, :]) & (key[None, :] < key[:, None])
    rank = jnp.sum(ahead.astype(jnp.int32), axis=1)
    fits = rank < total
    code = ((owners % n_inner) * per_dev + tile_row) * blocks + tile_col
    slots = jnp.arange(n_grp * total, dtype=jnp.int32)[:, None]
    mine = jnp.where(fits, step * total + rank, -1)[None, :] == slots
    index = jnp.sum(jnp.where(mine, order[None, :], 0), axis=1)
    theirs = jnp.where(fits, slab * total + rank, -1)[None, :] == slots
    codes = jnp.sum(jnp.where(theirs, code[None, :] + 1, 0), axis=1) - 1
    left_over = jnp.sum((~fits).astype(jnp.int32))

    where = jnp.stack([z, x]).astype(jnp.int32)

    def finish(parts):
        one, two = parts[:4], parts[4:]
        r1 = [lax.ppermute(one[s], "inner", along_x[s]) for s in (1, 3, 2)]
        r2 = [lax.ppermute(two[s], "inner", along_z[s]) for s in (1, 3, 2)]
        s1 = [one[0][q] + r1[0][q] + r1[1][q] + r1[2][q] for q in range(4)]
        s2 = [two[0][q] + r2[0][q] + r2[1][q] + r2[2][q] for q in range(4)]
        f1 = [lax.ppermute(s1[s], "inner", along_z[s]) for s in (1, 3, 2)]
        f2 = [lax.ppermute(s2[s], "inner", along_x[s]) for s in (1, 3, 2)]
        return [s1[0] + f1[0] + f1[1] + f1[2], s2[0] + f2[0] + f2[1] + f2[2]]

    p1, p3 = pack(integrals, index, ((1, 0, total), (3, 0, total)), total)
    r1, r3 = lax.ppermute(p1, "grp", along_y[1]), lax.ppermute(p3, "grp", along_y[3])
    p2, p4, p0 = pack(integrals, index, ((2, 0, FIRST), (2, FIRST, total), (0, 0, total)), total)
    r2, r4 = lax.ppermute(p2, "grp", along_y[2]), lax.ppermute(p4, "grp", along_y[2])
    codes, _ = lax.optimization_barrier((codes, p4))
    note = jnp.concatenate(
        [
            jnp.broadcast_to(codes.reshape(n_grp, 1, total), (n_grp, n_inner, total)),
            jnp.broadcast_to(left_over, (n_grp, n_inner, 1)),
        ],
        axis=2,
    ).astype(jnp.float32)
    note = lax.all_to_all(note.reshape(devices, total + 1), AXES, split_axis=0, concat_axis=0, tiled=True)
    overflow = jnp.sum(note[:, total]) > 0.5
    note = note[:, :total].reshape(n_grp, n_inner // 2, 2, total)
    note = lax.dynamic_index_in_dim(note, inner // 2, axis=1, keepdims=False)
    note = jnp.stack([lax.dynamic_index_in_dim(note, (grp - s + n_grp) % n_grp, axis=0, keepdims=False) for s in range(4)])
    note = jnp.stack([lax.dynamic_index_in_dim(note, core, axis=1, keepdims=False), lax.dynamic_index_in_dim(note, 1 - core, axis=1, keepdims=False)])
    note = note.astype(jnp.int32)

    def codes_of(steps, lo, hi):
        return jnp.concatenate([note[side, s, lo:hi] for side in range(2) for s in steps])

    def with_other(tiles):
        return [*tiles, *[lax.ppermute(t, "inner", across) for t in tiles]]

    (acc,) = ladder(codes_of((0, 1, 3), 0, total), where, amp, None, with_other([p0, gate(r1, note), gate(r3, note)]), False, blocks, 2 * 10**8)
    (acc,) = ladder(codes_of((2,), 0, FIRST), where, amp, acc, with_other([gate(r2, acc)]), False, blocks, 10**8)
    parts = ladder(codes_of((2,), FIRST, total), where, amp, acc, with_other([gate(r4, acc)]), True, blocks, 10**8)
    pieces = finish(parts)
    out = jnp.concatenate(pieces, axis=1)

    def with_rest(out):
        rest = jnp.where(fits[:, None, None], 0.0, integrals)
        return add(out, slow_part(amplitude, rest, tile_owner, tile_row, tile_col))

    return lax.cond(overflow, with_rest, lambda out: out, out)


def solution(mesh):
    placed = (P(AXES, None), P(AXES, None, None), P(AXES, None), P(AXES), P(AXES))
    return jax.shard_map(per_device, mesh=mesh, in_specs=placed, out_specs=P(AXES, None), check_vma=False)
```

```python
import functools

import jax
import jax.numpy as jnp
from jax import lax
from jax.experimental import pallas as pl
from jax.experimental.pallas import tpu as pltpu
from jax.sharding import PartitionSpec as P

TILE = 128
SLOTS = 40
FIRST = 30
VMEM = 60 * 1024 * 1024
AXES = ("grp", "inner")


def slow_part(amplitude, integrals, tile_owner, tile_row, tile_col):
    n_grp, n_inner = lax.axis_size("grp"), lax.axis_size("inner")
    devices = n_grp * n_inner
    count, size = integrals.shape[:2]
    blocks = amplitude.shape[1] // size
    per_dev = blocks // n_inner
    capacity = max(2, 2 * count // devices)
    owners = tile_owner[:, 0]
    order = jnp.arange(count, dtype=jnp.int32)
    same = (owners[:, None] == owners[None, :]) & (order[None, :] < order[:, None])
    slot = owners * capacity + jnp.sum(same.astype(jnp.int32), axis=1)
    position = (tile_row * blocks + tile_col).astype(jnp.float32)
    tiles = jnp.zeros((devices * capacity, size, size), jnp.float32).at[slot].set(integrals)
    place = jnp.zeros((devices * capacity,), jnp.float32).at[slot].set(position)
    tiles, place = (
        lax.all_to_all(tiles, AXES, split_axis=0, concat_axis=0, tiled=True),
        lax.all_to_all(place, AXES, split_axis=0, concat_axis=0, tiled=True),
    )
    dense = jnp.zeros((per_dev * blocks, size, size), jnp.float32).at[place.astype(jnp.int32)].add(tiles)
    dense = dense.reshape(per_dev, blocks, size, size).transpose(0, 2, 1, 3).reshape(per_dev * size, blocks * size)
    slab = lax.all_to_all(amplitude, "inner", split_axis=1, concat_axis=0, tiled=True)
    return lax.psum_scatter(
        jnp.dot(slab, dense, precision=lax.Precision.HIGHEST, preferred_element_type=jnp.float32),
        "inner",
        scatter_dimension=0,
        tiled=True,
    )


def pack_kernel(spans, total, index, tiles, *refs):
    outs, sems = refs[: len(spans)], refs[-1]
    for at, (which, lo, hi) in enumerate(spans):

        def issue(k, _):
            pltpu.make_async_copy(tiles.at[index[which * total + lo + k]], outs[at].at[k], sems.at[at]).start()
            return 0

        lax.fori_loop(0, hi - lo, issue, 0)
    for at, (_, lo, hi) in enumerate(spans):
        pltpu.make_async_copy(tiles.at[pl.ds(0, hi - lo)], outs[at], sems.at[at]).wait()


def pack(integrals, index, spans, total):
    return pl.pallas_call(
        functools.partial(pack_kernel, spans, total),
        out_shape=[jax.ShapeDtypeStruct((hi - lo, TILE, TILE), jnp.float32) for _, lo, hi in spans],
        in_specs=[pl.BlockSpec(memory_space=pltpu.SMEM), pl.BlockSpec(memory_space=pl.ANY)],
        out_specs=[pl.BlockSpec(memory_space=pltpu.VMEM)] * len(spans),
        scratch_shapes=[pltpu.SemaphoreType.DMA((len(spans),))],
        compiler_params=pltpu.CompilerParams(vmem_limit_bytes=VMEM),
        cost_estimate=pl.CostEstimate(flops=0, bytes_accessed=1000, transcendentals=0),
    )(index, integrals)


def add_kernel(one, two, out):
    out[...] = one[...] + two[...]


def add(one, two):
    return pl.pallas_call(add_kernel, out_shape=jax.ShapeDtypeStruct(one.shape, one.dtype))(one, two)


def gate_kernel(*refs):
    pass


def gate(value, *after):
    any_spec = pl.BlockSpec(memory_space=pl.ANY)
    return pl.pallas_call(
        gate_kernel,
        out_shape=jax.ShapeDtypeStruct(value.shape, value.dtype),
        in_specs=[any_spec] * (1 + len(after)),
        out_specs=any_spec,
        input_output_aliases={0: 0},
    )(value, *after)


def split(value):
    high = value.astype(jnp.bfloat16)
    return high, (value - high.astype(jnp.float32)).astype(jnp.bfloat16)


def ladder_kernel(counts, blocks, has_acc, last, *refs):
    refs, lists = list(refs), len(counts)
    code, where, amp = refs[:3]
    del refs[:3]
    acc_in = refs.pop(0) if has_acc else None
    tiles = refs[:lists]
    del refs[:lists]
    acc_out = None if last else refs.pop(0)
    parts = [refs.pop(0) for _ in range(10)] if last else []
    tile_v = refs[:lists]
    amp_v, acc_v, amp_sem, acc_sem, tile_sem, out_sem = refs[lists:]

    z, x = where[0], where[1]
    for sx in range(4):
        for sz in range(4):
            source = lax.rem(z + sz, 4) * 4 + lax.rem(x + sx, 4)
            pltpu.make_async_copy(amp.at[source], amp_v.at[sx * 4 + sz], amp_sem).start()
    if has_acc:
        acc_copy = pltpu.make_async_copy(acc_in, acc_v, acc_sem)
        acc_copy.start()
    copies = [pltpu.make_async_copy(tiles[k], tile_v[k], tile_sem.at[k]) for k in range(lists)]
    for copy in copies:
        copy.start()
    if has_acc:
        acc_copy.wait()
    else:
        acc_v[...] = jnp.zeros_like(acc_v)
    pltpu.make_async_copy(amp, amp_v, amp_sem).wait()

    for k in range(lists):
        copies[k].wait()
        base = sum(counts[:k])

        def pair(j, _):
            places = [code[base + 2 * j], code[base + 2 * j + 1]]

            @pl.when(jnp.maximum(*places) >= 0)
            def _():
                terms = []
                for half, place in enumerate(places):
                    held = jnp.maximum(place, 0)
                    row = pl.multiple_of((held // blocks) * TILE, TILE)
                    col = pl.multiple_of(lax.rem(held, blocks) * TILE, TILE)
                    a_hi, a_lo = split(amp_v[:, :, pl.ds(row, TILE)].reshape(16 * 8, TILE))
                    t_hi, t_lo = split(jnp.where(place >= 0, tile_v[k][2 * j + half], 0.0))
                    left = jnp.concatenate([a_hi, a_lo], axis=1)
                    right = jnp.concatenate([t_hi, t_lo], axis=1)
                    both = jnp.dot(left, jnp.concatenate([right, right], axis=0), preferred_element_type=jnp.float32)
                    terms.append((col, (both[:, :TILE] + both[:, TILE:]).reshape(4, 4, 8, TILE)))
                for col, term in terms:
                    acc_v[:, :, :, pl.ds(col, TILE)] += term

            return 0

        lax.fori_loop(0, counts[k] // 2, pair, 0)

    if last:
        half = blocks * TILE // 2
        one, two = pl.ds(0, half), pl.ds(half, half)
        sources = [acc_v.at[2, pl.ds(0, 2), :, one], acc_v.at[2, pl.ds(2, 2), :, one]]
        sources += [acc_v.at[pl.ds(0, 2), 2, :, two], acc_v.at[pl.ds(2, 2), 2, :, two]]
        sources += [acc_v.at[s, :, :, one] for s in (1, 3, 0)] + [acc_v.at[:, s, :, two] for s in (1, 3, 0)]
        done = [pltpu.make_async_copy(source, part, out_sem.at[i]) for i, (source, part) in enumerate(zip(sources, parts))]
    else:
        done = [pltpu.make_async_copy(acc_v, acc_out, out_sem.at[0])]
    for copy in done:
        copy.start()
    for copy in done:
        copy.wait()


def ladder(code, where, amp, acc, tiles, last, blocks, guess):
    counts = tuple(t.shape[0] for t in tiles)
    any_spec, smem = pl.BlockSpec(memory_space=pl.ANY), pl.BlockSpec(memory_space=pltpu.SMEM)
    if last:
        shapes = [jax.ShapeDtypeStruct((n, 8, blocks * TILE // 2), jnp.float32) for n in (2,) * 4 + (4,) * 6]
    else:
        shapes = [jax.ShapeDtypeStruct((4, 4, 8, blocks * TILE), jnp.float32)]
    given = [code, where, amp] + ([] if acc is None else [acc]) + list(tiles)
    return pl.pallas_call(
        functools.partial(ladder_kernel, counts, blocks, acc is not None, last),
        out_shape=shapes,
        in_specs=[smem, smem] + [any_spec] * (len(given) - 2),
        out_specs=[any_spec] * len(shapes),
        scratch_shapes=[
            *[pltpu.VMEM((n, TILE, TILE), jnp.float32) for n in counts],
            pltpu.VMEM((16, 8, blocks * TILE), jnp.float32),
            pltpu.VMEM((4, 4, 8, blocks * TILE), jnp.float32),
            pltpu.SemaphoreType.DMA,
            pltpu.SemaphoreType.DMA,
            pltpu.SemaphoreType.DMA((len(tiles),)),
            pltpu.SemaphoreType.DMA((10,)),
        ],
        compiler_params=pltpu.CompilerParams(vmem_limit_bytes=VMEM),
        cost_estimate=pl.CostEstimate(flops=0, bytes_accessed=guess, transcendentals=0),
    )(*given)


def per_device(amplitude, integrals, tile_owner, tile_row, tile_col):
    n_grp, n_inner = lax.axis_size("grp"), lax.axis_size("inner")
    devices = n_grp * n_inner
    rows, width = amplitude.shape
    count = integrals.shape[0]
    blocks = width // TILE
    per_dev = blocks // n_inner
    total = SLOTS
    grp, inner = lax.axis_index("grp"), lax.axis_index("inner")
    z, x, core = inner // 8, (inner // 2) % 4, inner % 2

    def at(z, x, core):
        return (z % 4) * 8 + (x % 4) * 2 + core

    every = [(a, b, c) for a in range(4) for b in range(4) for c in range(2)]
    along_x = {s: [(at(a, b, c), at(a, b + s, c)) for a, b, c in every] for s in (1, 2, 3)}
    along_z = {s: [(at(a, b, c), at(a + s, b, c)) for a, b, c in every] for s in (1, 2, 3)}
    along_y = {s: [(i, (i + s) % n_grp) for i in range(n_grp)] for s in (1, 2, 3)}
    across = [(i, i ^ 1) for i in range(n_inner)]
    same_core = [[at(a, b, c) for a in range(4) for b in range(4)] for c in range(2)]

    amp = lax.all_gather(amplitude, "inner", axis=0, axis_index_groups=same_core)

    owners = tile_owner[:, 0]
    slab = owners // n_inner
    step = (slab - grp + n_grp) % n_grp
    order = jnp.arange(count, dtype=jnp.int32)
    key = tile_col * count + order
    ahead = (slab[:, None] == slab[None, :]) & (key[None, :] < key[:, None])
    rank = jnp.sum(ahead.astype(jnp.int32), axis=1)
    fits = rank < total
    code = ((owners % n_inner) * per_dev + tile_row) * blocks + tile_col
    slots = jnp.arange(n_grp * total, dtype=jnp.int32)[:, None]
    mine = jnp.where(fits, step * total + rank, -1)[None, :] == slots
    index = jnp.sum(jnp.where(mine, order[None, :], 0), axis=1)
    theirs = jnp.where(fits, slab * total + rank, -1)[None, :] == slots
    codes = jnp.sum(jnp.where(theirs, code[None, :] + 1, 0), axis=1) - 1
    left_over = jnp.sum((~fits).astype(jnp.int32))

    where = jnp.stack([z, x]).astype(jnp.int32)

    def finish(parts):
        x_up, x_down, z_up, z_down = parts[:4]
        got_xu, got_xd = lax.ppermute(x_up, "inner", along_x[1]), lax.ppermute(x_down, "inner", along_x[3])
        got_zu, got_zd = lax.ppermute(z_up, "inner", along_z[1]), lax.ppermute(z_down, "inner", along_z[3])

        def onward(near_up, near_down, got_up, got_down):
            up = jnp.concatenate([near_up[:2] + got_up, near_up[2:]], axis=0)
            down = jnp.concatenate([near_down[:2], near_down[2:] + got_down], axis=0)
            return up, down

        x_up, x_down = onward(parts[4], parts[5], got_xu, got_xd)
        z_up, z_down = onward(parts[7], parts[8], got_zu, got_zd)
        got_xu, got_xd = lax.ppermute(x_up, "inner", along_x[1]), lax.ppermute(x_down, "inner", along_x[3])
        got_zu, got_zd = lax.ppermute(z_up, "inner", along_z[1]), lax.ppermute(z_down, "inner", along_z[3])
        s1 = [parts[6][q] + got_xu[q] + got_xd[q] for q in range(4)]
        s2 = [parts[9][q] + got_zu[q] + got_zd[q] for q in range(4)]
        f1 = [lax.ppermute(s1[s], "inner", along_z[s]) for s in (1, 3, 2)]
        f2 = [lax.ppermute(s2[s], "inner", along_x[s]) for s in (1, 3, 2)]
        return [s1[0] + f1[0] + f1[1] + f1[2], s2[0] + f2[0] + f2[1] + f2[2]]

    p1, p3 = pack(integrals, index, ((1, 0, total), (3, 0, total)), total)
    r1, r3 = lax.ppermute(p1, "grp", along_y[1]), lax.ppermute(p3, "grp", along_y[3])
    p2, p4, p0 = pack(integrals, index, ((2, 0, FIRST), (2, FIRST, total), (0, 0, total)), total)
    r2, r4 = lax.ppermute(p2, "grp", along_y[2]), lax.ppermute(p4, "grp", along_y[2])
    codes, _ = lax.optimization_barrier((codes, p4))
    note = jnp.concatenate(
        [
            jnp.broadcast_to(codes.reshape(n_grp, 1, total), (n_grp, n_inner, total)),
            jnp.broadcast_to(left_over, (n_grp, n_inner, 1)),
        ],
        axis=2,
    ).astype(jnp.float32)
    note = lax.all_to_all(note.reshape(devices, total + 1), AXES, split_axis=0, concat_axis=0, tiled=True)
    overflow = jnp.sum(note[:, total]) > 0.5
    note = note[:, :total].reshape(n_grp, n_inner // 2, 2, total)
    note = lax.dynamic_index_in_dim(note, inner // 2, axis=1, keepdims=False)
    note = jnp.stack([lax.dynamic_index_in_dim(note, (grp - s + n_grp) % n_grp, axis=0, keepdims=False) for s in range(4)])
    note = jnp.stack([lax.dynamic_index_in_dim(note, core, axis=1, keepdims=False), lax.dynamic_index_in_dim(note, 1 - core, axis=1, keepdims=False)])
    note = note.astype(jnp.int32)

    def codes_of(steps, lo, hi):
        return jnp.concatenate([note[side, s, lo:hi] for side in range(2) for s in steps])

    def with_other(tiles):
        return [*tiles, *[lax.ppermute(t, "inner", across) for t in tiles]]

    (acc,) = ladder(codes_of((0, 1, 3), 0, total), where, amp, None, with_other([p0, gate(r1, note), gate(r3, note)]), False, blocks, 1000)
    (acc,) = ladder(codes_of((2,), 0, FIRST), where, amp, acc, with_other([gate(r2, acc)]), False, blocks, 1000)
    parts = ladder(codes_of((2,), FIRST, total), where, amp, acc, with_other([gate(r4, acc)]), True, blocks, 10**8)
    pieces = finish(parts)
    out = jnp.concatenate(pieces, axis=1)

    def with_rest(out):
        rest = jnp.where(fits[:, None, None], 0.0, integrals)
        return add(out, slow_part(amplitude, rest, tile_owner, tile_row, tile_col))

    return lax.cond(overflow, with_rest, lambda out: out, out)


def solution(mesh):
    placed = (P(AXES, None), P(AXES, None, None), P(AXES, None), P(AXES), P(AXES))
    return jax.shard_map(per_device, mesh=mesh, in_specs=placed, out_specs=P(AXES, None), check_vma=False)
```

```python
import functools

import jax
import jax.numpy as jnp
from jax import lax
from jax.experimental import pallas as pl
from jax.experimental.pallas import tpu as pltpu
from jax.sharding import PartitionSpec as P

TILE = 128
SLOTS = 40
FIRST = 30
VMEM = 24 * 1024 * 1024
AXES = ("grp", "inner")


def slow_part(amplitude, integrals, tile_owner, tile_row, tile_col):
    n_grp, n_inner = lax.axis_size("grp"), lax.axis_size("inner")
    devices = n_grp * n_inner
    count, size = integrals.shape[:2]
    blocks = amplitude.shape[1] // size
    per_dev = blocks // n_inner
    capacity = max(2, 2 * count // devices)
    owners = tile_owner[:, 0]
    order = jnp.arange(count, dtype=jnp.int32)
    same = (owners[:, None] == owners[None, :]) & (order[None, :] < order[:, None])
    slot = owners * capacity + jnp.sum(same.astype(jnp.int32), axis=1)
    position = (tile_row * blocks + tile_col).astype(jnp.float32)
    tiles = jnp.zeros((devices * capacity, size, size), jnp.float32).at[slot].set(integrals)
    place = jnp.zeros((devices * capacity,), jnp.float32).at[slot].set(position)
    tiles, place = (
        lax.all_to_all(tiles, AXES, split_axis=0, concat_axis=0, tiled=True),
        lax.all_to_all(place, AXES, split_axis=0, concat_axis=0, tiled=True),
    )
    dense = jnp.zeros((per_dev * blocks, size, size), jnp.float32).at[place.astype(jnp.int32)].add(tiles)
    dense = dense.reshape(per_dev, blocks, size, size).transpose(0, 2, 1, 3).reshape(per_dev * size, blocks * size)
    slab = lax.all_to_all(amplitude, "inner", split_axis=1, concat_axis=0, tiled=True)
    return lax.psum_scatter(
        jnp.dot(slab, dense, precision=lax.Precision.HIGHEST, preferred_element_type=jnp.float32),
        "inner",
        scatter_dimension=0,
        tiled=True,
    )


def pack_kernel(spans, total, index, tiles, *refs):
    outs, sems = refs[: len(spans)], refs[-1]
    for at, (which, lo, hi) in enumerate(spans):

        def issue(k, _):
            pltpu.make_async_copy(tiles.at[index[which * total + lo + k]], outs[at].at[k], sems.at[at]).start()
            return 0

        lax.fori_loop(0, hi - lo, issue, 0)
    for at, (_, lo, hi) in enumerate(spans):
        pltpu.make_async_copy(tiles.at[pl.ds(0, hi - lo)], outs[at], sems.at[at]).wait()


def pack(integrals, index, spans, total):
    return pl.pallas_call(
        functools.partial(pack_kernel, spans, total),
        out_shape=[jax.ShapeDtypeStruct((hi - lo, TILE, TILE), jnp.float32) for _, lo, hi in spans],
        in_specs=[pl.BlockSpec(memory_space=pltpu.SMEM), pl.BlockSpec(memory_space=pl.ANY)],
        out_specs=[pl.BlockSpec(memory_space=pltpu.VMEM)] * len(spans),
        scratch_shapes=[pltpu.SemaphoreType.DMA((len(spans),))],
        compiler_params=pltpu.CompilerParams(vmem_limit_bytes=16 * 2**20),
        cost_estimate=pl.CostEstimate(flops=0, bytes_accessed=1000, transcendentals=0),
    )(index, integrals)


def add_kernel(one, two, out):
    out[...] = one[...] + two[...]


def add(one, two):
    return pl.pallas_call(add_kernel, out_shape=jax.ShapeDtypeStruct(one.shape, one.dtype))(one, two)


def gate_kernel(*refs):
    pass


def gate(value, *after):
    any_spec = pl.BlockSpec(memory_space=pl.ANY)
    return pl.pallas_call(
        gate_kernel,
        out_shape=jax.ShapeDtypeStruct(value.shape, value.dtype),
        in_specs=[any_spec] * (1 + len(after)),
        out_specs=any_spec,
        input_output_aliases={0: 0},
        compiler_params=pltpu.CompilerParams(vmem_limit_bytes=2**17),
    )(value, *after)


def split(value):
    high = value.astype(jnp.bfloat16)
    return high, (value - high.astype(jnp.float32)).astype(jnp.bfloat16)


def arrange_kernel(where, amp, out, sem):
    z, x = where[0], where[1]
    for sx in range(4):
        for sz in range(4):
            source = lax.rem(z + sz, 4) * 4 + lax.rem(x + sx, 4)
            pltpu.make_async_copy(amp.at[source], out.at[sx * 4 + sz], sem).start()
    pltpu.make_async_copy(amp, out, sem).wait()


def arrange(where, amp):
    return pl.pallas_call(
        arrange_kernel,
        out_shape=pltpu.VMEM(amp.shape, amp.dtype),
        in_specs=[pl.BlockSpec(memory_space=pltpu.SMEM), pl.BlockSpec(memory_space=pl.ANY)],
        out_specs=pl.BlockSpec(memory_space=pltpu.VMEM),
        scratch_shapes=[pltpu.SemaphoreType.DMA],
        compiler_params=pltpu.CompilerParams(vmem_limit_bytes=2**20),
        cost_estimate=pl.CostEstimate(flops=0, bytes_accessed=1000, transcendentals=0),
    )(where, amp)


def ladder_kernel(counts, blocks, first, last, *refs):
    refs, lists = list(refs), len(counts)
    code, amp_v = refs[:2]
    del refs[:2]
    acc_v = None if first else refs.pop(0)
    tiles = refs[:lists]
    del refs[:lists]
    if last:
        parts = [refs.pop(0) for _ in range(10)]
    else:
        acc_v = refs.pop(0)
        token = refs.pop(0)
        token[...] = jnp.zeros_like(token)
    tile_v = refs[:lists]
    tile_sem, out_sem = refs[lists:]

    copies = [pltpu.make_async_copy(tiles[k], tile_v[k], tile_sem.at[k]) for k in range(lists)]
    for copy in copies:
        copy.start()
    if first:
        acc_v[...] = jnp.zeros_like(acc_v)

    for k in range(lists):
        copies[k].wait()
        base = sum(counts[:k])

        def pair(j, _):
            places = [code[base + 2 * j], code[base + 2 * j + 1]]

            @pl.when(jnp.maximum(*places) >= 0)
            def _():
                terms = []
                for half, place in enumerate(places):
                    held = jnp.maximum(place, 0)
                    row = pl.multiple_of((held // blocks) * TILE, TILE)
                    col = pl.multiple_of(lax.rem(held, blocks) * TILE, TILE)
                    a_hi, a_lo = split(amp_v[:, :, pl.ds(row, TILE)].reshape(16 * 8, TILE))
                    t_hi, t_lo = split(jnp.where(place >= 0, tile_v[k][2 * j + half], 0.0))
                    left = jnp.concatenate([a_hi, a_lo], axis=1)
                    right = jnp.concatenate([t_hi, t_lo], axis=1)
                    both = jnp.dot(left, jnp.concatenate([right, right], axis=0), preferred_element_type=jnp.float32)
                    terms.append((col, (both[:, :TILE] + both[:, TILE:]).reshape(4, 4, 8, TILE)))
                for col, term in terms:
                    acc_v[:, :, :, pl.ds(col, TILE)] += term

            return 0

        lax.fori_loop(0, counts[k] // 2, pair, 0)

    if last:
        half = blocks * TILE // 2
        one, two = pl.ds(0, half), pl.ds(half, half)
        sources = [acc_v.at[2, pl.ds(0, 2), :, one], acc_v.at[2, pl.ds(2, 2), :, one]]
        sources += [acc_v.at[pl.ds(0, 2), 2, :, two], acc_v.at[pl.ds(2, 2), 2, :, two]]
        sources += [acc_v.at[s, :, :, one] for s in (1, 3, 0)] + [acc_v.at[:, s, :, two] for s in (1, 3, 0)]
        done = [pltpu.make_async_copy(source, part, out_sem.at[i]) for i, (source, part) in enumerate(zip(sources, parts))]
        for copy in done:
            copy.start()
        for copy in done:
            copy.wait()


def keep(value):
    return pltpu.with_memory_space_constraint(value, pltpu.VMEM)


def ladder(code, amp, acc, tiles, last, blocks):
    counts = tuple(t.shape[0] for t in tiles)
    any_spec, smem, vmem = [pl.BlockSpec(memory_space=m) for m in (pl.ANY, pltpu.SMEM, pltpu.VMEM)]
    held = [] if acc is None else [acc]
    if last:
        shapes = [pltpu.HBM((n, 8, blocks * TILE // 2), jnp.float32) for n in (2,) * 4 + (4,) * 6]
    else:
        shapes = [pltpu.VMEM((4, 4, 8, blocks * TILE), jnp.float32), jax.ShapeDtypeStruct((8, TILE), jnp.float32)]
    return pl.pallas_call(
        functools.partial(ladder_kernel, counts, blocks, acc is None, last),
        out_shape=shapes,
        in_specs=[smem, vmem] + [vmem] * len(held) + [any_spec] * len(tiles),
        out_specs=[any_spec] * len(shapes) if last else [vmem, vmem],
        scratch_shapes=[
            *[pltpu.VMEM((n, TILE, TILE), jnp.float32) for n in counts],
            pltpu.SemaphoreType.DMA((len(tiles),)),
            pltpu.SemaphoreType.DMA((10,)),
        ],
        input_output_aliases={2: 0} if held and not last else {},
        compiler_params=pltpu.CompilerParams(vmem_limit_bytes=VMEM),
        cost_estimate=pl.CostEstimate(flops=0, bytes_accessed=1000, transcendentals=0),
    )(code, keep(amp), *[keep(h) for h in held], *tiles)


def per_device(amplitude, integrals, tile_owner, tile_row, tile_col):
    n_grp, n_inner = lax.axis_size("grp"), lax.axis_size("inner")
    devices = n_grp * n_inner
    rows, width = amplitude.shape
    count = integrals.shape[0]
    blocks = width // TILE
    per_dev = blocks // n_inner
    total = SLOTS
    grp, inner = lax.axis_index("grp"), lax.axis_index("inner")
    z, x, core = inner // 8, (inner // 2) % 4, inner % 2

    def at(z, x, core):
        return (z % 4) * 8 + (x % 4) * 2 + core

    every = [(a, b, c) for a in range(4) for b in range(4) for c in range(2)]
    along_x = {s: [(at(a, b, c), at(a, b + s, c)) for a, b, c in every] for s in (1, 2, 3)}
    along_z = {s: [(at(a, b, c), at(a + s, b, c)) for a, b, c in every] for s in (1, 2, 3)}
    along_y = {s: [(i, (i + s) % n_grp) for i in range(n_grp)] for s in (1, 2, 3)}
    across = [(i, i ^ 1) for i in range(n_inner)]
    same_core = [[at(a, b, c) for a in range(4) for b in range(4)] for c in range(2)]

    amp = lax.all_gather(amplitude, "inner", axis=0, axis_index_groups=same_core)

    owners = tile_owner[:, 0]
    slab = owners // n_inner
    step = (slab - grp + n_grp) % n_grp
    order = jnp.arange(count, dtype=jnp.int32)
    key = tile_col * count + order
    ahead = (slab[:, None] == slab[None, :]) & (key[None, :] < key[:, None])
    rank = jnp.sum(ahead.astype(jnp.int32), axis=1)
    fits = rank < total
    code = ((owners % n_inner) * per_dev + tile_row) * blocks + tile_col
    slots = jnp.arange(n_grp * total, dtype=jnp.int32)[:, None]
    mine = jnp.where(fits, step * total + rank, -1)[None, :] == slots
    index = jnp.sum(jnp.where(mine, order[None, :], 0), axis=1)
    theirs = jnp.where(fits, slab * total + rank, -1)[None, :] == slots
    codes = jnp.sum(jnp.where(theirs, code[None, :] + 1, 0), axis=1) - 1
    left_over = jnp.sum((~fits).astype(jnp.int32))

    where = jnp.stack([z, x]).astype(jnp.int32)

    def finish(parts):
        x_up, x_down, z_up, z_down = parts[:4]
        got_xu, got_xd = lax.ppermute(x_up, "inner", along_x[1]), lax.ppermute(x_down, "inner", along_x[3])
        got_zu, got_zd = lax.ppermute(z_up, "inner", along_z[1]), lax.ppermute(z_down, "inner", along_z[3])

        def onward(near_up, near_down, got_up, got_down):
            up = jnp.concatenate([near_up[:2] + got_up, near_up[2:]], axis=0)
            down = jnp.concatenate([near_down[:2], near_down[2:] + got_down], axis=0)
            return up, down

        x_up, x_down = onward(parts[4], parts[5], got_xu, got_xd)
        z_up, z_down = onward(parts[7], parts[8], got_zu, got_zd)
        got_xu, got_xd = lax.ppermute(x_up, "inner", along_x[1]), lax.ppermute(x_down, "inner", along_x[3])
        got_zu, got_zd = lax.ppermute(z_up, "inner", along_z[1]), lax.ppermute(z_down, "inner", along_z[3])
        s1 = [parts[6][q] + got_xu[q] + got_xd[q] for q in range(4)]
        s2 = [parts[9][q] + got_zu[q] + got_zd[q] for q in range(4)]
        f1 = [lax.ppermute(s1[s], "inner", along_z[s]) for s in (1, 3, 2)]
        f2 = [lax.ppermute(s2[s], "inner", along_x[s]) for s in (1, 3, 2)]
        return [s1[0] + f1[0] + f1[1] + f1[2], s2[0] + f2[0] + f2[1] + f2[2]]

    p1, p3 = pack(integrals, index, ((1, 0, total), (3, 0, total)), total)
    r1, r3 = lax.ppermute(p1, "grp", along_y[1]), lax.ppermute(p3, "grp", along_y[3])
    p2, p4, p0 = pack(integrals, index, ((2, 0, FIRST), (2, FIRST, total), (0, 0, total)), total)
    r2, r4 = lax.ppermute(p2, "grp", along_y[2]), lax.ppermute(p4, "grp", along_y[2])
    codes, _ = lax.optimization_barrier((codes, p4))
    note = jnp.concatenate(
        [
            jnp.broadcast_to(codes.reshape(n_grp, 1, total), (n_grp, n_inner, total)),
            jnp.broadcast_to(left_over, (n_grp, n_inner, 1)),
        ],
        axis=2,
    ).astype(jnp.float32)
    note = lax.all_to_all(note.reshape(devices, total + 1), AXES, split_axis=0, concat_axis=0, tiled=True)
    overflow = jnp.sum(note[:, total]) > 0.5
    note = note[:, :total].reshape(n_grp, n_inner // 2, 2, total)
    note = lax.dynamic_index_in_dim(note, inner // 2, axis=1, keepdims=False)
    note = jnp.stack([lax.dynamic_index_in_dim(note, (grp - s + n_grp) % n_grp, axis=0, keepdims=False) for s in range(4)])
    note = jnp.stack([lax.dynamic_index_in_dim(note, core, axis=1, keepdims=False), lax.dynamic_index_in_dim(note, 1 - core, axis=1, keepdims=False)])
    note = note.astype(jnp.int32)

    def codes_of(steps, lo, hi):
        return jnp.concatenate([note[side, s, lo:hi] for side in range(2) for s in steps])

    def with_other(tiles):
        return [*tiles, *[lax.ppermute(t, "inner", across) for t in tiles]]

    amp = arrange(where, amp)
    acc, token = ladder(codes_of((0, 1, 3), 0, total), amp, None, with_other([p0, gate(r1, note), gate(r3, note)]), False, blocks)
    acc, token = ladder(codes_of((2,), 0, FIRST), amp, acc, with_other([gate(r2, token)]), False, blocks)
    parts = ladder(codes_of((2,), FIRST, total), amp, acc, with_other([gate(r4, token)]), True, blocks)
    pieces = finish(parts)
    out = jnp.concatenate(pieces, axis=1)

    def with_rest(out):
        rest = jnp.where(fits[:, None, None], 0.0, integrals)
        return add(out, slow_part(amplitude, rest, tile_owner, tile_row, tile_col))

    return lax.cond(overflow, with_rest, lambda out: out, out)


def solution(mesh):
    placed = (P(AXES, None), P(AXES, None, None), P(AXES, None), P(AXES), P(AXES))
    return jax.shard_map(per_device, mesh=mesh, in_specs=placed, out_specs=P(AXES, None), check_vma=False)
```

```python
import functools

import jax
import jax.numpy as jnp
from jax import lax
from jax.experimental import pallas as pl
from jax.experimental.pallas import tpu as pltpu
from jax.sharding import PartitionSpec as P

TILE = 128
SLOTS = 40
FIRST = 30
LOW = 64
GUESS = (80 * 10**6, 35 * 10**6, 20 * 10**6)
AXES = ("grp", "inner")


def slow_part(amplitude, integrals, tile_owner, tile_row, tile_col):
    n_grp, n_inner = lax.axis_size("grp"), lax.axis_size("inner")
    devices = n_grp * n_inner
    count, size = integrals.shape[:2]
    blocks = amplitude.shape[1] // size
    per_dev = blocks // n_inner
    capacity = max(2, 2 * count // devices)
    owners = tile_owner[:, 0]
    order = jnp.arange(count, dtype=jnp.int32)
    same = (owners[:, None] == owners[None, :]) & (order[None, :] < order[:, None])
    slot = owners * capacity + jnp.sum(same.astype(jnp.int32), axis=1)
    position = (tile_row * blocks + tile_col).astype(jnp.float32)
    tiles = jnp.zeros((devices * capacity, size, size), jnp.float32).at[slot].set(integrals)
    place = jnp.zeros((devices * capacity,), jnp.float32).at[slot].set(position)
    tiles, place = (
        lax.all_to_all(tiles, AXES, split_axis=0, concat_axis=0, tiled=True),
        lax.all_to_all(place, AXES, split_axis=0, concat_axis=0, tiled=True),
    )
    dense = jnp.zeros((per_dev * blocks, size, size), jnp.float32).at[place.astype(jnp.int32)].add(tiles)
    dense = dense.reshape(per_dev, blocks, size, size).transpose(0, 2, 1, 3).reshape(per_dev * size, blocks * size)
    slab = lax.all_to_all(amplitude, "inner", split_axis=1, concat_axis=0, tiled=True)
    return lax.psum_scatter(
        jnp.dot(slab, dense, precision=lax.Precision.HIGHEST, preferred_element_type=jnp.float32),
        "inner",
        scatter_dimension=0,
        tiled=True,
    )


def pack_kernel(spans, total, index, tiles, *refs):
    outs, sems = refs[: len(spans)], refs[-1]
    for at, (which, lo, hi) in enumerate(spans):

        def issue(k, _):
            pltpu.make_async_copy(tiles.at[index[which * total + lo + k]], outs[at].at[k], sems.at[at]).start()
            return 0

        lax.fori_loop(0, hi - lo, issue, 0)
    for at, (_, lo, hi) in enumerate(spans):
        pltpu.make_async_copy(tiles.at[pl.ds(0, hi - lo)], outs[at], sems.at[at]).wait()


def pack(integrals, index, spans, total):
    return pl.pallas_call(
        functools.partial(pack_kernel, spans, total),
        out_shape=[jax.ShapeDtypeStruct((hi - lo, TILE, TILE), jnp.float32) for _, lo, hi in spans],
        in_specs=[pl.BlockSpec(memory_space=pltpu.SMEM), pl.BlockSpec(memory_space=pl.ANY)],
        out_specs=[pl.BlockSpec(memory_space=pltpu.VMEM)] * len(spans),
        scratch_shapes=[pltpu.SemaphoreType.DMA((len(spans),))],
        compiler_params=pltpu.CompilerParams(vmem_limit_bytes=16 * 2**20),
        cost_estimate=pl.CostEstimate(flops=0, bytes_accessed=1000, transcendentals=0),
    )(index, integrals)


def add_kernel(one, two, out):
    out[...] = one[...] + two[...]


def total_kernel(*refs):
    out, width = refs[-1], refs[0].shape[1]
    for piece in range(len(refs) // 4):
        group = refs[piece * 4 : piece * 4 + 4]
        out[:, pl.ds(piece * width, width)] = (group[0][...] + group[1][...]) + (group[2][...] + group[3][...])


def small(kernel, shape, *values):
    return pl.pallas_call(
        kernel,
        out_shape=jax.ShapeDtypeStruct(shape, jnp.float32),
        compiler_params=pltpu.CompilerParams(vmem_limit_bytes=6 * 2**20),
    )(*values)


def gate_kernel(*refs):
    pass


def gate(value, *after):
    any_spec = pl.BlockSpec(memory_space=pl.ANY)
    return pl.pallas_call(
        gate_kernel,
        out_shape=jax.ShapeDtypeStruct(value.shape, value.dtype),
        in_specs=[any_spec] * (1 + len(after)),
        out_specs=any_spec,
        input_output_aliases={0: 0},
        compiler_params=pltpu.CompilerParams(vmem_limit_bytes=2**17),
    )(value, *after)


def split(value):
    high = value.astype(jnp.bfloat16)
    return high, (value - high.astype(jnp.float32)).astype(jnp.bfloat16)


def start_arranged(where, amp, out, sem):
    z, x = where[0], where[1]
    for sx in range(4):
        for sz in range(4):
            source = lax.rem(z + sz, 4) * 4 + lax.rem(x + sx, 4)
            pltpu.make_async_copy(amp.at[source], out.at[sx * 4 + sz], sem).start()


def arrange_kernel(where, amp, out, sem):
    start_arranged(where, amp, out, sem)
    pltpu.make_async_copy(amp, out, sem).wait()


def arrange(where, amp):
    return pl.pallas_call(
        arrange_kernel,
        out_shape=pltpu.VMEM(amp.shape, amp.dtype),
        in_specs=[pl.BlockSpec(memory_space=pltpu.SMEM), pl.BlockSpec(memory_space=pl.ANY)],
        out_specs=pl.BlockSpec(memory_space=pltpu.VMEM),
        scratch_shapes=[pltpu.SemaphoreType.DMA],
        compiler_params=pltpu.CompilerParams(vmem_limit_bytes=2**20),
        cost_estimate=pl.CostEstimate(flops=0, bytes_accessed=1000, transcendentals=0),
    )(where, amp)


def multiply(code, counts, tiles, tile_v, tile_sem, amp_v, acc_v, low, blocks):
    for k, count in enumerate(counts):
        pltpu.make_async_copy(tiles[k], tile_v[k], tile_sem.at[k]).wait()
        base = sum(counts[:k])

        def pair(j, _):
            places = [code[base + 2 * j], code[base + 2 * j + 1]]

            @pl.when(jnp.maximum(*places) >= 0)
            def _():
                terms = []
                for half, place in enumerate(places):
                    held = jnp.maximum(place, low)
                    row = pl.multiple_of((held // blocks) * TILE, TILE)
                    col = pl.multiple_of((lax.rem(held, blocks) - low) * TILE, TILE)
                    a_hi, a_lo = split(amp_v[:, :, pl.ds(row, TILE)].reshape(16 * 8, TILE))
                    t_hi, t_lo = split(jnp.where(place >= 0, tile_v[k][2 * j + half], 0.0))
                    left = jnp.concatenate([a_hi, a_lo], axis=1)
                    right = jnp.concatenate([t_hi, t_lo], axis=1)
                    both = jnp.dot(left, jnp.concatenate([right, right], axis=0), preferred_element_type=jnp.float32)
                    terms.append((col, (both[:, :TILE] + both[:, TILE:]).reshape(4, 4, 8, TILE)))
                for col, term in terms:
                    acc_v[:, :, :, pl.ds(col, TILE)] += term

            return 0

        lax.fori_loop(0, count // 2, pair, 0)


def part_copies(acc_v, width, parts, sem):
    half = width // 2
    one, two = pl.ds(0, half), pl.ds(half, half)
    sources = [acc_v.at[2, pl.ds(0, 2), :, one], acc_v.at[2, pl.ds(2, 2), :, one]]
    sources += [acc_v.at[pl.ds(0, 2), 2, :, two], acc_v.at[pl.ds(2, 2), 2, :, two]]
    sources += [acc_v.at[s, :, :, one] for s in (1, 3, 0)] + [acc_v.at[:, s, :, two] for s in (1, 3, 0)]
    return [pltpu.make_async_copy(source, part, sem.at[i]) for i, (source, part) in enumerate(zip(sources, parts))]


def ladder_kernel(step, counts, low, *refs):
    refs, lists = list(refs), len(counts)

    def take(n):
        taken = refs[:n]
        del refs[:n]
        return taken

    code, amp = take(2)
    where, acc_in = take(2) if step == 2 else (None, None)
    (acc_v,) = take(1) if step == 1 else (None,)
    tiles = take(lists)
    parts = take(10) if step else []
    (rest,) = take(1) if step == 1 else (None,)
    if step == 0:
        (acc_v,) = take(1)
    if step < 2:
        (token,) = take(1)
        token[...] = jnp.zeros_like(token)
    tile_v = take(lists)
    tile_sem, out_sem = take(2)
    for k in range(lists):
        pltpu.make_async_copy(tiles[k], tile_v[k], tile_sem.at[k]).start()
    amp_v = amp
    if step == 0:
        acc_v[...] = jnp.zeros_like(acc_v)
    if step == 2:
        amp_v, acc_v, held_sem = refs
        start_arranged(where, amp, amp_v, held_sem.at[0])
        acc_copy = pltpu.make_async_copy(acc_in, acc_v, held_sem.at[1])
        acc_copy.start()
        pltpu.make_async_copy(amp, amp_v, held_sem.at[0]).wait()
        acc_copy.wait()
    blocks = amp.shape[2] // TILE
    multiply(code, counts, tiles, tile_v, tile_sem, amp_v, acc_v, low if step == 2 else 0, blocks)
    done = part_copies(acc_v, acc_in.shape[3] if step == 2 else low * TILE, parts, out_sem) if step else []
    if step == 1:
        done.append(pltpu.make_async_copy(acc_v.at[:, :, :, pl.ds(low * TILE, (blocks - low) * TILE)], rest, out_sem.at[10]))
    for copy in done:
        copy.start()
    for copy in done:
        copy.wait()


def keep(value):
    return pltpu.with_memory_space_constraint(value, pltpu.VMEM)


def ladder(step, code, amp, held, tiles, blocks, guess):
    counts = tuple(t.shape[0] for t in tiles)
    any_spec, smem, vmem = [pl.BlockSpec(memory_space=m) for m in (pl.ANY, pltpu.SMEM, pltpu.VMEM)]
    width = ((blocks, LOW, blocks - LOW)[step]) * TILE
    token = jax.ShapeDtypeStruct((8, TILE), jnp.float32)
    parts = [pltpu.HBM((n, 8, width // 2), jnp.float32) for n in (2,) * 4 + (4,) * 6]
    if step == 0:
        given, into, shapes, specs = [keep(amp)], [vmem], [pltpu.VMEM((4, 4, 8, width), jnp.float32), token], [vmem] * 2
    elif step == 1:
        given, into = [keep(amp), keep(held)], [vmem] * 2
        shapes, specs = [*parts, pltpu.HBM((4, 4, 8, blocks * TILE - width), jnp.float32), token], [any_spec] * 11 + [vmem]
    else:
        given, into, shapes, specs = [amp, *held], [any_spec, smem, any_spec], parts, [any_spec] * 10
    scratch = [pltpu.VMEM((n, TILE, TILE), jnp.float32) for n in counts]
    scratch += [pltpu.SemaphoreType.DMA((len(tiles),)), pltpu.SemaphoreType.DMA((11,))]
    limit = 2**21 + sum(counts) * TILE * TILE * 4
    if step == 2:
        scratch += [pltpu.VMEM(amp.shape, jnp.float32), pltpu.VMEM((4, 4, 8, width), jnp.float32), pltpu.SemaphoreType.DMA((2,))]
        limit += 12 * 2**20
    return pl.pallas_call(
        functools.partial(ladder_kernel, step, counts, LOW),
        out_shape=shapes,
        in_specs=[smem] + into + [any_spec] * len(tiles),
        out_specs=specs,
        scratch_shapes=scratch,
        compiler_params=pltpu.CompilerParams(vmem_limit_bytes=limit),
        cost_estimate=pl.CostEstimate(flops=0, bytes_accessed=guess, transcendentals=0),
    )(code, *given, *tiles)


def per_device(amplitude, integrals, tile_owner, tile_row, tile_col):
    n_grp, n_inner = lax.axis_size("grp"), lax.axis_size("inner")
    devices = n_grp * n_inner
    rows, width = amplitude.shape
    count = integrals.shape[0]
    blocks = width // TILE
    per_dev = blocks // n_inner
    total = SLOTS
    grp, inner = lax.axis_index("grp"), lax.axis_index("inner")
    z, x, core = inner // 8, (inner // 2) % 4, inner % 2

    def at(z, x, core):
        return (z % 4) * 8 + (x % 4) * 2 + core

    every = [(a, b, c) for a in range(4) for b in range(4) for c in range(2)]
    along_x = {s: [(at(a, b, c), at(a, b + s, c)) for a, b, c in every] for s in (1, 2, 3)}
    along_z = {s: [(at(a, b, c), at(a + s, b, c)) for a, b, c in every] for s in (1, 2, 3)}
    along_y = {s: [(i, (i + s) % n_grp) for i in range(n_grp)] for s in (1, 2, 3)}
    across = [(i, i ^ 1) for i in range(n_inner)]
    same_core = [[at(a, b, c) for a in range(4) for b in range(4)] for c in range(2)]

    amp = lax.all_gather(amplitude, "inner", axis=0, axis_index_groups=same_core)

    owners = tile_owner[:, 0]
    slab = owners // n_inner
    step = (slab - grp + n_grp) % n_grp
    order = jnp.arange(count, dtype=jnp.int32)
    key = tile_col * count + order
    ahead = (slab[:, None] == slab[None, :]) & (key[None, :] < key[:, None])
    rank = jnp.sum(ahead.astype(jnp.int32), axis=1)
    fits = rank < jnp.where(tile_col < LOW, FIRST, total)
    code = ((owners % n_inner) * per_dev + tile_row) * blocks + tile_col
    slots = jnp.arange(n_grp * total, dtype=jnp.int32)[:, None]
    mine = jnp.where(fits, step * total + rank, -1)[None, :] == slots
    index = jnp.sum(jnp.where(mine, order[None, :], 0), axis=1)
    theirs = jnp.where(fits, slab * total + rank, -1)[None, :] == slots
    codes = jnp.sum(jnp.where(theirs, code[None, :] + 1, 0), axis=1) - 1
    left_over = jnp.sum((~fits).astype(jnp.int32))

    where = jnp.stack([z, x]).astype(jnp.int32)

    def finish(parts):
        x_up, x_down, z_up, z_down = parts[:4]
        got_xu, got_xd = lax.ppermute(x_up, "inner", along_x[1]), lax.ppermute(x_down, "inner", along_x[3])
        got_zu, got_zd = lax.ppermute(z_up, "inner", along_z[1]), lax.ppermute(z_down, "inner", along_z[3])

        def onward(near_up, near_down, got_up, got_down):
            up = jnp.concatenate([near_up[:2] + got_up, near_up[2:]], axis=0)
            down = jnp.concatenate([near_down[:2], near_down[2:] + got_down], axis=0)
            return up, down

        x_up, x_down = onward(parts[4], parts[5], got_xu, got_xd)
        z_up, z_down = onward(parts[7], parts[8], got_zu, got_zd)
        got_xu, got_xd = lax.ppermute(x_up, "inner", along_x[1]), lax.ppermute(x_down, "inner", along_x[3])
        got_zu, got_zd = lax.ppermute(z_up, "inner", along_z[1]), lax.ppermute(z_down, "inner", along_z[3])
        s1 = [parts[6][q] + got_xu[q] + got_xd[q] for q in range(4)]
        s2 = [parts[9][q] + got_zu[q] + got_zd[q] for q in range(4)]
        f1 = [lax.ppermute(s1[s], "inner", along_z[s]) for s in (1, 3, 2)]
        f2 = [lax.ppermute(s2[s], "inner", along_x[s]) for s in (1, 3, 2)]
        return [s1[0], *f1, s2[0], *f2]

    p1, p3 = pack(integrals, index, ((1, 0, FIRST), (3, 0, FIRST)), total)
    r1, r3 = lax.ppermute(p1, "grp", along_y[1]), lax.ppermute(p3, "grp", along_y[3])
    p2, p4, p5, p6, p0 = pack(integrals, index, ((2, 0, FIRST), (1, FIRST, total), (2, FIRST, total), (3, FIRST, total), (0, 0, total)), total)
    r2 = lax.ppermute(p2, "grp", along_y[2])
    late = [lax.ppermute(p, "grp", along_y[s]) for p, s in ((p4, 1), (p6, 3), (p5, 2))]
    codes, _ = lax.optimization_barrier((codes, p2))
    note = jnp.concatenate(
        [
            jnp.broadcast_to(codes.reshape(n_grp, 1, total), (n_grp, n_inner, total)),
            jnp.broadcast_to(left_over, (n_grp, n_inner, 1)),
        ],
        axis=2,
    ).astype(jnp.float32)
    note = lax.all_to_all(note.reshape(devices, total + 1), AXES, split_axis=0, concat_axis=0, tiled=True)
    overflow = jnp.sum(note[:, total]) > 0.5
    note = note[:, :total].reshape(n_grp, n_inner // 2, 2, total)
    note = lax.dynamic_index_in_dim(note, inner // 2, axis=1, keepdims=False)
    note = jnp.stack([lax.dynamic_index_in_dim(note, (grp - s + n_grp) % n_grp, axis=0, keepdims=False) for s in range(4)])
    note = jnp.stack([lax.dynamic_index_in_dim(note, core, axis=1, keepdims=False), lax.dynamic_index_in_dim(note, 1 - core, axis=1, keepdims=False)])
    note = note.astype(jnp.int32)

    def codes_of(*pieces):
        return jnp.concatenate([note[side, s, lo:hi] for side in range(2) for s, lo, hi in pieces])

    def with_other(tiles):
        return [*tiles, *[lax.ppermute(t, "inner", across) for t in tiles]]

    held = arrange(where, amp)
    acc, token = ladder(0, codes_of((0, 0, total), (1, 0, FIRST), (3, 0, FIRST)), held, None, with_other([p0, gate(r1, note), gate(r3, note)]), blocks, GUESS[0])
    *parts, acc, token = ladder(1, codes_of((2, 0, FIRST)), held, acc, with_other([gate(r2, token)]), blocks, GUESS[1])
    pieces = finish(parts)
    late = with_other([gate(r, token) for r in late])
    parts = ladder(2, codes_of((1, FIRST, total), (3, FIRST, total), (2, FIRST, total)), amp, (where, acc), late, blocks, GUESS[2])
    pieces += finish(parts)
    out = small(total_kernel, (rows, width), *pieces)

    def with_rest(out):
        rest = jnp.where(fits[:, None, None], 0.0, integrals)
        return small(add_kernel, out.shape, out, slow_part(amplitude, rest, tile_owner, tile_row, tile_col))

    return lax.cond(overflow, with_rest, lambda out: out, out)


def solution(mesh):
    placed = (P(AXES, None), P(AXES, None, None), P(AXES, None), P(AXES), P(AXES))
    return jax.shard_map(per_device, mesh=mesh, in_specs=placed, out_specs=P(AXES, None), check_vma=False)
```

```python
import functools

import jax
import jax.numpy as jnp
from jax import lax
from jax.experimental import pallas as pl
from jax.experimental.pallas import tpu as pltpu
from jax.sharding import PartitionSpec as P

TILE = 128
SLOTS = 40
FIRST = 30
LOW = 64
GUESS = (80 * 10**6, 35 * 10**6, 20 * 10**6)
AXES = ("grp", "inner")


def slow_part(amplitude, integrals, tile_owner, tile_row, tile_col):
    n_grp, n_inner = lax.axis_size("grp"), lax.axis_size("inner")
    devices = n_grp * n_inner
    count, size = integrals.shape[:2]
    blocks = amplitude.shape[1] // size
    per_dev = blocks // n_inner
    capacity = max(2, 2 * count // devices)
    owners = tile_owner[:, 0]
    order = jnp.arange(count, dtype=jnp.int32)
    same = (owners[:, None] == owners[None, :]) & (order[None, :] < order[:, None])
    slot = owners * capacity + jnp.sum(same.astype(jnp.int32), axis=1)
    position = (tile_row * blocks + tile_col).astype(jnp.float32)
    tiles = jnp.zeros((devices * capacity, size, size), jnp.float32).at[slot].set(integrals)
    place = jnp.zeros((devices * capacity,), jnp.float32).at[slot].set(position)
    tiles, place = (
        lax.all_to_all(tiles, AXES, split_axis=0, concat_axis=0, tiled=True),
        lax.all_to_all(place, AXES, split_axis=0, concat_axis=0, tiled=True),
    )
    dense = jnp.zeros((per_dev * blocks, size, size), jnp.float32).at[place.astype(jnp.int32)].add(tiles)
    dense = dense.reshape(per_dev, blocks, size, size).transpose(0, 2, 1, 3).reshape(per_dev * size, blocks * size)
    slab = lax.all_to_all(amplitude, "inner", split_axis=1, concat_axis=0, tiled=True)
    return lax.psum_scatter(
        jnp.dot(slab, dense, precision=lax.Precision.HIGHEST, preferred_element_type=jnp.float32),
        "inner",
        scatter_dimension=0,
        tiled=True,
    )


def pack_kernel(spans, total, index, tiles, *refs):
    outs, sems = refs[: len(spans)], refs[-1]
    for at, (which, lo, hi) in enumerate(spans):

        def issue(k, _):
            pltpu.make_async_copy(tiles.at[index[which * total + lo + k]], outs[at].at[k], sems.at[at]).start()
            return 0

        lax.fori_loop(0, hi - lo, issue, 0)
    for at, (_, lo, hi) in enumerate(spans):
        pltpu.make_async_copy(tiles.at[pl.ds(0, hi - lo)], outs[at], sems.at[at]).wait()


def pack(integrals, index, spans, total):
    return pl.pallas_call(
        functools.partial(pack_kernel, spans, total),
        out_shape=[jax.ShapeDtypeStruct((hi - lo, TILE, TILE), jnp.float32) for _, lo, hi in spans],
        in_specs=[pl.BlockSpec(memory_space=pltpu.SMEM), pl.BlockSpec(memory_space=pl.ANY)],
        out_specs=[pl.BlockSpec(memory_space=pltpu.VMEM)] * len(spans),
        scratch_shapes=[pltpu.SemaphoreType.DMA((len(spans),))],
        compiler_params=pltpu.CompilerParams(vmem_limit_bytes=16 * 2**20),
        cost_estimate=pl.CostEstimate(flops=0, bytes_accessed=1000, transcendentals=0),
    )(index, in_hbm(integrals))


def pack_late_kernel(total, index, me, tiles, out, sem):
    steps, count = out.shape[:2]
    for step in range(steps):
        there = lax.rem(me[0] + step, steps)

        def issue(k, _):
            pltpu.make_async_copy(tiles.at[index[step * total + total - count + k]], out.at[there, k], sem.at[step]).start()
            return 0

        lax.fori_loop(0, count, issue, 0)
    for step in range(steps):
        pltpu.make_async_copy(tiles.at[pl.ds(0, count)], out.at[step], sem.at[step]).wait()


def pack_late(integrals, index, me, total, steps, count):
    smem = pl.BlockSpec(memory_space=pltpu.SMEM)
    return pl.pallas_call(
        functools.partial(pack_late_kernel, total),
        out_shape=jax.ShapeDtypeStruct((steps, count, TILE, TILE), jnp.float32),
        in_specs=[smem, smem, pl.BlockSpec(memory_space=pl.ANY)],
        out_specs=pl.BlockSpec(memory_space=pltpu.VMEM),
        scratch_shapes=[pltpu.SemaphoreType.DMA((steps,))],
        compiler_params=pltpu.CompilerParams(vmem_limit_bytes=8 * 2**20),
        cost_estimate=pl.CostEstimate(flops=0, bytes_accessed=1000, transcendentals=0),
    )(index, me, in_hbm(integrals))


def in_hbm(value):
    return pltpu.with_memory_space_constraint(value, pltpu.HBM)


def add_kernel(one, two, out):
    out[...] = one[...] + two[...]


def total_kernel(*refs):
    out, width = refs[-1], refs[0].shape[1]
    for piece in range(len(refs) // 4):
        group = refs[piece * 4 : piece * 4 + 4]
        out[:, pl.ds(piece * width, width)] = (group[0][...] + group[1][...]) + (group[2][...] + group[3][...])


def small(kernel, shape, *values):
    return pl.pallas_call(
        kernel,
        out_shape=jax.ShapeDtypeStruct(shape, jnp.float32),
        compiler_params=pltpu.CompilerParams(vmem_limit_bytes=6 * 2**20),
    )(*values)


def gate_kernel(*refs):
    pass


def gate(value, *after):
    any_spec = pl.BlockSpec(memory_space=pl.ANY)
    return pl.pallas_call(
        gate_kernel,
        out_shape=jax.ShapeDtypeStruct(value.shape, value.dtype),
        in_specs=[any_spec] * (1 + len(after)),
        out_specs=any_spec,
        input_output_aliases={0: 0},
        compiler_params=pltpu.CompilerParams(vmem_limit_bytes=2**17),
    )(value, *after)


def split(value):
    high = value.astype(jnp.bfloat16)
    return high, (value - high.astype(jnp.float32)).astype(jnp.bfloat16)


def start_arranged(where, amp, out, sem):
    z, x = where[0], where[1]
    for sx in range(4):
        for sz in range(4):
            source = lax.rem(z + sz, 4) * 4 + lax.rem(x + sx, 4)
            pltpu.make_async_copy(amp.at[source], out.at[sx * 4 + sz], sem).start()


def arrange_kernel(where, amp, out, sem):
    start_arranged(where, amp, out, sem)
    pltpu.make_async_copy(amp, out, sem).wait()


def arrange(where, amp):
    return pl.pallas_call(
        arrange_kernel,
        out_shape=pltpu.VMEM(amp.shape, amp.dtype),
        in_specs=[pl.BlockSpec(memory_space=pltpu.SMEM), pl.BlockSpec(memory_space=pl.ANY)],
        out_specs=pl.BlockSpec(memory_space=pltpu.VMEM),
        scratch_shapes=[pltpu.SemaphoreType.DMA],
        compiler_params=pltpu.CompilerParams(vmem_limit_bytes=2**20),
        cost_estimate=pl.CostEstimate(flops=0, bytes_accessed=1000, transcendentals=0),
    )(where, in_hbm(amp))


def multiply(code, counts, tiles, tile_v, tile_sem, amp_v, acc_v, low, blocks):
    for k, count in enumerate(counts):
        pltpu.make_async_copy(tiles[k], tile_v[k], tile_sem.at[k]).wait()
        base = sum(counts[:k])

        def pair(j, _):
            places = [code[base + 2 * j], code[base + 2 * j + 1]]

            @pl.when(jnp.maximum(*places) >= 0)
            def _():
                terms = []
                for half, place in enumerate(places):
                    held = jnp.maximum(place, low)
                    row = pl.multiple_of((held // blocks) * TILE, TILE)
                    col = pl.multiple_of((lax.rem(held, blocks) - low) * TILE, TILE)
                    a_hi, a_lo = split(amp_v[:, :, pl.ds(row, TILE)].reshape(16 * 8, TILE))
                    t_hi, t_lo = split(jnp.where(place >= 0, tile_v[k][2 * j + half], 0.0))
                    left = jnp.concatenate([a_hi, a_lo], axis=1)
                    right = jnp.concatenate([t_hi, t_lo], axis=1)
                    both = jnp.dot(left, jnp.concatenate([right, right], axis=0), preferred_element_type=jnp.float32)
                    terms.append((col, (both[:, :TILE] + both[:, TILE:]).reshape(4, 4, 8, TILE)))
                for col, term in terms:
                    acc_v[:, :, :, pl.ds(col, TILE)] += term

            return 0

        lax.fori_loop(0, count // 2, pair, 0)


def part_copies(acc_v, width, parts, sem):
    half = width // 2
    one, two = pl.ds(0, half), pl.ds(half, half)
    sources = [acc_v.at[2, pl.ds(0, 2), :, one], acc_v.at[2, pl.ds(2, 2), :, one]]
    sources += [acc_v.at[pl.ds(0, 2), 2, :, two], acc_v.at[pl.ds(2, 2), 2, :, two]]
    sources += [acc_v.at[s, :, :, one] for s in (1, 3, 0)] + [acc_v.at[:, s, :, two] for s in (1, 3, 0)]
    return [pltpu.make_async_copy(source, part, sem.at[i]) for i, (source, part) in enumerate(zip(sources, parts))]


def ladder_kernel(step, counts, low, *refs):
    refs, lists = list(refs), len(counts)

    def take(n):
        taken = refs[:n]
        del refs[:n]
        return taken

    code, amp = take(2)
    where, acc_in = take(2) if step == 2 else (None, None)
    (acc_v,) = take(1) if step == 1 else (None,)
    tiles = take(lists)
    parts = take(10) if step else []
    (rest,) = take(1) if step == 1 else (None,)
    if step == 0:
        (acc_v,) = take(1)
    if step < 2:
        (token,) = take(1)
        token[...] = jnp.zeros_like(token)
    tile_v = take(lists)
    tile_sem, out_sem = take(2)
    for k in range(lists):
        pltpu.make_async_copy(tiles[k], tile_v[k], tile_sem.at[k]).start()
    amp_v = amp
    if step == 0:
        acc_v[...] = jnp.zeros_like(acc_v)
    if step == 2:
        amp_v, acc_v, held_sem = refs
        start_arranged(where, amp, amp_v, held_sem.at[0])
        acc_copy = pltpu.make_async_copy(acc_in, acc_v, held_sem.at[1])
        acc_copy.start()
        pltpu.make_async_copy(amp, amp_v, held_sem.at[0]).wait()
        acc_copy.wait()
    blocks = amp.shape[2] // TILE
    multiply(code, counts, tiles, tile_v, tile_sem, amp_v, acc_v, low if step == 2 else 0, blocks)
    done = part_copies(acc_v, acc_in.shape[3] if step == 2 else low * TILE, parts, out_sem) if step else []
    if step == 1:
        done.append(pltpu.make_async_copy(acc_v.at[:, :, :, pl.ds(low * TILE, (blocks - low) * TILE)], rest, out_sem.at[10]))
    for copy in done:
        copy.start()
    for copy in done:
        copy.wait()


def keep(value):
    return pltpu.with_memory_space_constraint(value, pltpu.VMEM)


def ladder(step, code, amp, held, tiles, blocks, guess):
    counts = tuple(t.shape[0] for t in tiles)
    any_spec, smem, vmem = [pl.BlockSpec(memory_space=m) for m in (pl.ANY, pltpu.SMEM, pltpu.VMEM)]
    width = ((blocks, LOW, blocks - LOW)[step]) * TILE
    token = jax.ShapeDtypeStruct((8, TILE), jnp.float32)
    parts = [pltpu.HBM((n, 8, width // 2), jnp.float32) for n in (2,) * 4 + (4,) * 6]
    if step == 0:
        given, into, shapes, specs = [keep(amp)], [vmem], [pltpu.VMEM((4, 4, 8, width), jnp.float32), token], [vmem] * 2
    elif step == 1:
        given, into = [keep(amp), keep(held)], [vmem] * 2
        shapes, specs = [*parts, pltpu.HBM((4, 4, 8, blocks * TILE - width), jnp.float32), token], [any_spec] * 11 + [vmem]
    else:
        given, into, shapes, specs = [in_hbm(amp), *held], [any_spec, smem, any_spec], parts, [any_spec] * 10
    scratch = [pltpu.VMEM((n, TILE, TILE), jnp.float32) for n in counts]
    scratch += [pltpu.SemaphoreType.DMA((len(tiles),)), pltpu.SemaphoreType.DMA((11,))]
    limit = 2**21 + sum(counts) * TILE * TILE * 4
    if step == 2:
        scratch += [pltpu.VMEM(amp.shape, jnp.float32), pltpu.VMEM((4, 4, 8, width), jnp.float32), pltpu.SemaphoreType.DMA((2,))]
        limit += 12 * 2**20
    return pl.pallas_call(
        functools.partial(ladder_kernel, step, counts, LOW),
        out_shape=shapes,
        in_specs=[smem] + into + [any_spec] * len(tiles),
        out_specs=specs,
        scratch_shapes=scratch,
        compiler_params=pltpu.CompilerParams(vmem_limit_bytes=limit),
        cost_estimate=pl.CostEstimate(flops=0, bytes_accessed=guess, transcendentals=0),
    )(code, *given, *tiles)


def per_device(amplitude, integrals, tile_owner, tile_row, tile_col):
    n_grp, n_inner = lax.axis_size("grp"), lax.axis_size("inner")
    devices = n_grp * n_inner
    rows, width = amplitude.shape
    count = integrals.shape[0]
    blocks = width // TILE
    per_dev = blocks // n_inner
    total = SLOTS
    grp, inner = lax.axis_index("grp"), lax.axis_index("inner")
    z, x, core = inner // 8, (inner // 2) % 4, inner % 2

    def at(z, x, core):
        return (z % 4) * 8 + (x % 4) * 2 + core

    every = [(a, b, c) for a in range(4) for b in range(4) for c in range(2)]
    along_x = {s: [(at(a, b, c), at(a, b + s, c)) for a, b, c in every] for s in (1, 2, 3)}
    along_z = {s: [(at(a, b, c), at(a + s, b, c)) for a, b, c in every] for s in (1, 2, 3)}
    along_y = {s: [(i, (i + s) % n_grp) for i in range(n_grp)] for s in (1, 2, 3)}
    across = [(i, i ^ 1) for i in range(n_inner)]
    same_core = [[at(a, b, c) for a in range(4) for b in range(4)] for c in range(2)]

    amp = lax.all_gather(amplitude, "inner", axis=0, axis_index_groups=same_core)

    owners = tile_owner[:, 0]
    slab = owners // n_inner
    step = (slab - grp + n_grp) % n_grp
    order = jnp.arange(count, dtype=jnp.int32)
    key = tile_col * count + order
    ahead = (slab[:, None] == slab[None, :]) & (key[None, :] < key[:, None])
    rank = jnp.sum(ahead.astype(jnp.int32), axis=1)
    fits = rank < jnp.where(tile_col < LOW, FIRST, total)
    code = ((owners % n_inner) * per_dev + tile_row) * blocks + tile_col
    slots = jnp.arange(n_grp * total, dtype=jnp.int32)[:, None]
    mine = jnp.where(fits, step * total + rank, -1)[None, :] == slots
    index = jnp.sum(jnp.where(mine, order[None, :], 0), axis=1)
    theirs = jnp.where(fits, slab * total + rank, -1)[None, :] == slots
    codes = jnp.sum(jnp.where(theirs, code[None, :] + 1, 0), axis=1) - 1
    left_over = jnp.sum((~fits).astype(jnp.int32))

    where = jnp.stack([z, x]).astype(jnp.int32)

    def finish(parts):
        x_up, x_down, z_up, z_down = parts[:4]
        got_xu, got_xd = lax.ppermute(x_up, "inner", along_x[1]), lax.ppermute(x_down, "inner", along_x[3])
        got_zu, got_zd = lax.ppermute(z_up, "inner", along_z[1]), lax.ppermute(z_down, "inner", along_z[3])

        def onward(near_up, near_down, got_up, got_down):
            up = jnp.concatenate([near_up[:2] + got_up, near_up[2:]], axis=0)
            down = jnp.concatenate([near_down[:2], near_down[2:] + got_down], axis=0)
            return up, down

        x_up, x_down = onward(parts[4], parts[5], got_xu, got_xd)
        z_up, z_down = onward(parts[7], parts[8], got_zu, got_zd)
        got_xu, got_xd = lax.ppermute(x_up, "inner", along_x[1]), lax.ppermute(x_down, "inner", along_x[3])
        got_zu, got_zd = lax.ppermute(z_up, "inner", along_z[1]), lax.ppermute(z_down, "inner", along_z[3])
        s1 = [parts[6][q] + got_xu[q] + got_xd[q] for q in range(4)]
        s2 = [parts[9][q] + got_zu[q] + got_zd[q] for q in range(4)]
        f1 = [lax.ppermute(s1[s], "inner", along_z[s]) for s in (1, 3, 2)]
        f2 = [lax.ppermute(s2[s], "inner", along_x[s]) for s in (1, 3, 2)]
        return [s1[0], *f1, s2[0], *f2], (x_up, x_down, z_up, z_down)

    p1, p3 = pack(integrals, index, ((1, 0, FIRST), (3, 0, FIRST)), total)
    r1, r3 = lax.ppermute(p1, "grp", along_y[1]), lax.ppermute(p3, "grp", along_y[3])
    p2, p0 = pack(integrals, index, ((2, 0, FIRST), (0, 0, FIRST)), total)
    r2 = lax.ppermute(p2, "grp", along_y[2])
    late = pack_late(integrals, index, grp.reshape(1).astype(jnp.int32), total, n_grp, total - FIRST)
    codes, _ = lax.optimization_barrier((codes, p2))
    note = jnp.concatenate(
        [
            jnp.broadcast_to(codes.reshape(n_grp, 1, total), (n_grp, n_inner, total)),
            jnp.broadcast_to(left_over, (n_grp, n_inner, 1)),
        ],
        axis=2,
    ).astype(jnp.float32)
    note = lax.all_to_all(note.reshape(devices, total + 1), AXES, split_axis=0, concat_axis=0, tiled=True)
    overflow = jnp.sum(note[:, total]) > 0.5
    note = note[:, :total].reshape(n_grp, n_inner // 2, 2, total)
    note = lax.dynamic_index_in_dim(note, inner // 2, axis=1, keepdims=False)
    note = jnp.stack([lax.dynamic_index_in_dim(note, core, axis=1, keepdims=False), lax.dynamic_index_in_dim(note, 1 - core, axis=1, keepdims=False)])
    note = note.astype(jnp.int32)
    late_codes = note[:, :, FIRST:].reshape(-1)
    note = jnp.stack([lax.dynamic_index_in_dim(note, (grp - s + n_grp) % n_grp, axis=1, keepdims=False) for s in range(4)], axis=1)

    def codes_of(*pieces):
        return jnp.concatenate([note[side, s, lo:hi] for side in range(2) for s, lo, hi in pieces])

    def with_other(tiles):
        return [*tiles, *[lax.ppermute(t, "inner", across) for t in tiles]]

    late_sent = late
    late = lax.all_to_all(late, "grp", split_axis=0, concat_axis=0, tiled=True).reshape(-1, TILE, TILE)
    held = arrange(where, amp)
    acc, token = ladder(0, codes_of((0, 0, FIRST), (1, 0, FIRST), (3, 0, FIRST)), held, None, with_other([p0, gate(r1, note, late_sent), gate(r3, note)]), blocks, GUESS[0])
    *parts, acc, token = ladder(1, codes_of((2, 0, FIRST)), held, acc, with_other([gate(r2, token)]), blocks, GUESS[1])
    pieces, under_way = finish(parts)
    parts = ladder(2, late_codes, amp, (where, acc), with_other([gate(late, token, *under_way)]), blocks, GUESS[2])
    pieces += finish(parts)[0]
    out = small(total_kernel, (rows, width), *pieces)

    def with_rest(out):
        rest = jnp.where(fits[:, None, None], 0.0, integrals)
        return small(add_kernel, out.shape, out, slow_part(amplitude, rest, tile_owner, tile_row, tile_col))

    return lax.cond(overflow, with_rest, lambda out: out, out)


def solution(mesh):
    placed = (P(AXES, None), P(AXES, None, None), P(AXES, None), P(AXES), P(AXES))
    return jax.shard_map(per_device, mesh=mesh, in_specs=placed, out_specs=P(AXES, None), check_vma=False)
```

```python
import functools

import jax
import jax.numpy as jnp
from jax import lax
from jax.experimental import pallas as pl
from jax.experimental.pallas import tpu as pltpu
from jax.sharding import PartitionSpec as P

TILE = 128
SLOTS = 40
FIRST = 30
EARLY = 20
VMEM = 24 * 1024 * 1024
AXES = ("grp", "inner")


def slow_part(amplitude, integrals, tile_owner, tile_row, tile_col):
    n_grp, n_inner = lax.axis_size("grp"), lax.axis_size("inner")
    devices = n_grp * n_inner
    count, size = integrals.shape[:2]
    blocks = amplitude.shape[1] // size
    per_dev = blocks // n_inner
    capacity = max(2, 2 * count // devices)
    owners = tile_owner[:, 0]
    order = jnp.arange(count, dtype=jnp.int32)
    same = (owners[:, None] == owners[None, :]) & (order[None, :] < order[:, None])
    slot = owners * capacity + jnp.sum(same.astype(jnp.int32), axis=1)
    position = (tile_row * blocks + tile_col).astype(jnp.float32)
    tiles = jnp.zeros((devices * capacity, size, size), jnp.float32).at[slot].set(integrals)
    place = jnp.zeros((devices * capacity,), jnp.float32).at[slot].set(position)
    tiles, place = (
        lax.all_to_all(tiles, AXES, split_axis=0, concat_axis=0, tiled=True),
        lax.all_to_all(place, AXES, split_axis=0, concat_axis=0, tiled=True),
    )
    dense = jnp.zeros((per_dev * blocks, size, size), jnp.float32).at[place.astype(jnp.int32)].add(tiles)
    dense = dense.reshape(per_dev, blocks, size, size).transpose(0, 2, 1, 3).reshape(per_dev * size, blocks * size)
    slab = lax.all_to_all(amplitude, "inner", split_axis=1, concat_axis=0, tiled=True)
    return lax.psum_scatter(
        jnp.dot(slab, dense, precision=lax.Precision.HIGHEST, preferred_element_type=jnp.float32),
        "inner",
        scatter_dimension=0,
        tiled=True,
    )


def pack_kernel(spans, total, index, tiles, *refs):
    outs, sems = refs[: len(spans)], refs[-1]
    for at, (which, lo, hi) in enumerate(spans):

        def issue(k, _):
            pltpu.make_async_copy(tiles.at[index[which * total + lo + k]], outs[at].at[k], sems.at[at]).start()
            return 0

        lax.fori_loop(0, hi - lo, issue, 0)
    for at, (_, lo, hi) in enumerate(spans):
        pltpu.make_async_copy(tiles.at[pl.ds(0, hi - lo)], outs[at], sems.at[at]).wait()


def pack(integrals, index, spans, total):
    return pl.pallas_call(
        functools.partial(pack_kernel, spans, total),
        out_shape=[jax.ShapeDtypeStruct((hi - lo, TILE, TILE), jnp.float32) for _, lo, hi in spans],
        in_specs=[pl.BlockSpec(memory_space=pltpu.SMEM), pl.BlockSpec(memory_space=pl.ANY)],
        out_specs=[pl.BlockSpec(memory_space=pltpu.VMEM)] * len(spans),
        scratch_shapes=[pltpu.SemaphoreType.DMA((len(spans),))],
        compiler_params=pltpu.CompilerParams(vmem_limit_bytes=16 * 2**20),
        cost_estimate=pl.CostEstimate(flops=0, bytes_accessed=1000, transcendentals=0),
    )(index, integrals)


def add_kernel(one, two, out):
    out[...] = one[...] + two[...]


def add(one, two):
    return pl.pallas_call(add_kernel, out_shape=jax.ShapeDtypeStruct(one.shape, one.dtype))(one, two)


def gate_kernel(*refs):
    pass


def gate(value, *after):
    any_spec = pl.BlockSpec(memory_space=pl.ANY)
    return pl.pallas_call(
        gate_kernel,
        out_shape=jax.ShapeDtypeStruct(value.shape, value.dtype),
        in_specs=[any_spec] * (1 + len(after)),
        out_specs=any_spec,
        input_output_aliases={0: 0},
        compiler_params=pltpu.CompilerParams(vmem_limit_bytes=2**17),
    )(value, *after)


def split(value):
    high = value.astype(jnp.bfloat16)
    return high, (value - high.astype(jnp.float32)).astype(jnp.bfloat16)


def arrange_kernel(where, amp, out, sem):
    z, x = where[0], where[1]
    for sx in range(4):
        for sz in range(4):
            source = lax.rem(z + sz, 4) * 4 + lax.rem(x + sx, 4)
            pltpu.make_async_copy(amp.at[source], out.at[sx * 4 + sz], sem).start()
    pltpu.make_async_copy(amp, out, sem).wait()


def arrange(where, amp):
    return pl.pallas_call(
        arrange_kernel,
        out_shape=pltpu.VMEM(amp.shape, amp.dtype),
        in_specs=[pl.BlockSpec(memory_space=pltpu.SMEM), pl.BlockSpec(memory_space=pl.ANY)],
        out_specs=pl.BlockSpec(memory_space=pltpu.VMEM),
        scratch_shapes=[pltpu.SemaphoreType.DMA],
        compiler_params=pltpu.CompilerParams(vmem_limit_bytes=2**20),
        cost_estimate=pl.CostEstimate(flops=0, bytes_accessed=1000, transcendentals=0),
    )(where, amp)


def ladder_kernel(counts, blocks, first, last, *refs):
    refs, lists = list(refs), len(counts)
    code, amp_v = refs[:2]
    del refs[:2]
    acc_v = None if first else refs.pop(0)
    tiles = refs[:lists]
    del refs[:lists]
    if last:
        parts = [refs.pop(0) for _ in range(10)]
    else:
        acc_v = refs.pop(0)
        token = refs.pop(0)
        token[...] = jnp.zeros_like(token)
    tile_v = refs[:lists]
    tile_sem, out_sem = refs[lists:]

    copies = [pltpu.make_async_copy(tiles[k], tile_v[k], tile_sem.at[k]) for k in range(lists)]
    for copy in copies:
        copy.start()
    if first:
        acc_v[...] = jnp.zeros_like(acc_v)

    for k in range(lists):
        copies[k].wait()
        base = sum(counts[:k])

        def pair(j, _):
            places = [code[base + 2 * j], code[base + 2 * j + 1]]

            @pl.when(jnp.maximum(*places) >= 0)
            def _():
                terms = []
                for half, place in enumerate(places):
                    held = jnp.maximum(place, 0)
                    row = pl.multiple_of((held // blocks) * TILE, TILE)
                    col = pl.multiple_of(lax.rem(held, blocks) * TILE, TILE)
                    a_hi, a_lo = split(amp_v[:, :, pl.ds(row, TILE)].reshape(16 * 8, TILE))
                    t_hi, t_lo = split(jnp.where(place >= 0, tile_v[k][2 * j + half], 0.0))
                    left = jnp.concatenate([a_hi, a_lo], axis=1)
                    right = jnp.concatenate([t_hi, t_lo], axis=1)
                    both = jnp.dot(left, jnp.concatenate([right, right], axis=0), preferred_element_type=jnp.float32)
                    terms.append((col, (both[:, :TILE] + both[:, TILE:]).reshape(4, 4, 8, TILE)))
                for col, term in terms:
                    acc_v[:, :, :, pl.ds(col, TILE)] += term

            return 0

        lax.fori_loop(0, counts[k] // 2, pair, 0)

    if last:
        half = blocks * TILE // 2
        one, two = pl.ds(0, half), pl.ds(half, half)
        sources = [acc_v.at[2, pl.ds(0, 2), :, one], acc_v.at[2, pl.ds(2, 2), :, one]]
        sources += [acc_v.at[pl.ds(0, 2), 2, :, two], acc_v.at[pl.ds(2, 2), 2, :, two]]
        sources += [acc_v.at[s, :, :, one] for s in (1, 3, 0)] + [acc_v.at[:, s, :, two] for s in (1, 3, 0)]
        done = [pltpu.make_async_copy(source, part, out_sem.at[i]) for i, (source, part) in enumerate(zip(sources, parts))]
        for copy in done:
            copy.start()
        for copy in done:
            copy.wait()


def keep(value):
    return pltpu.with_memory_space_constraint(value, pltpu.VMEM)


def ladder(code, amp, acc, tiles, last, blocks):
    counts = tuple(t.shape[0] for t in tiles)
    any_spec, smem, vmem = [pl.BlockSpec(memory_space=m) for m in (pl.ANY, pltpu.SMEM, pltpu.VMEM)]
    held = [] if acc is None else [acc]
    if last:
        shapes = [pltpu.HBM((n, 8, blocks * TILE // 2), jnp.float32) for n in (2,) * 4 + (4,) * 6]
    else:
        shapes = [pltpu.VMEM((4, 4, 8, blocks * TILE), jnp.float32), jax.ShapeDtypeStruct((8, TILE), jnp.float32)]
    return pl.pallas_call(
        functools.partial(ladder_kernel, counts, blocks, acc is None, last),
        out_shape=shapes,
        in_specs=[smem, vmem] + [vmem] * len(held) + [any_spec] * len(tiles),
        out_specs=[any_spec] * len(shapes) if last else [vmem, vmem],
        scratch_shapes=[
            *[pltpu.VMEM((n, TILE, TILE), jnp.float32) for n in counts],
            pltpu.SemaphoreType.DMA((len(tiles),)),
            pltpu.SemaphoreType.DMA((10,)),
        ],
        input_output_aliases={2: 0} if held and not last else {},
        compiler_params=pltpu.CompilerParams(vmem_limit_bytes=VMEM),
        cost_estimate=pl.CostEstimate(flops=0, bytes_accessed=1000, transcendentals=0),
    )(code, keep(amp), *[keep(h) for h in held], *tiles)


def per_device(amplitude, integrals, tile_owner, tile_row, tile_col):
    n_grp, n_inner = lax.axis_size("grp"), lax.axis_size("inner")
    devices = n_grp * n_inner
    rows, width = amplitude.shape
    count = integrals.shape[0]
    blocks = width // TILE
    per_dev = blocks // n_inner
    total = SLOTS
    grp, inner = lax.axis_index("grp"), lax.axis_index("inner")
    z, x, core = inner // 8, (inner // 2) % 4, inner % 2

    def at(z, x, core):
        return (z % 4) * 8 + (x % 4) * 2 + core

    every = [(a, b, c) for a in range(4) for b in range(4) for c in range(2)]
    along_x = {s: [(at(a, b, c), at(a, b + s, c)) for a, b, c in every] for s in (1, 2, 3)}
    along_z = {s: [(at(a, b, c), at(a + s, b, c)) for a, b, c in every] for s in (1, 2, 3)}
    along_y = {s: [(i, (i + s) % n_grp) for i in range(n_grp)] for s in (1, 2, 3)}
    across = [(i, i ^ 1) for i in range(n_inner)]
    same_core = [[at(a, b, c) for a in range(4) for b in range(4)] for c in range(2)]

    amp = lax.all_gather(amplitude, "inner", axis=0, axis_index_groups=same_core)

    owners = tile_owner[:, 0]
    slab = owners // n_inner
    step = (slab - grp + n_grp) % n_grp
    order = jnp.arange(count, dtype=jnp.int32)
    key = tile_col * count + order
    ahead = (slab[:, None] == slab[None, :]) & (key[None, :] < key[:, None])
    rank = jnp.sum(ahead.astype(jnp.int32), axis=1)
    fits = rank < total
    code = ((owners % n_inner) * per_dev + tile_row) * blocks + tile_col
    slots = jnp.arange(n_grp * total, dtype=jnp.int32)[:, None]
    mine = jnp.where(fits, step * total + rank, -1)[None, :] == slots
    index = jnp.sum(jnp.where(mine, order[None, :], 0), axis=1)
    theirs = jnp.where(fits, slab * total + rank, -1)[None, :] == slots
    codes = jnp.sum(jnp.where(theirs, code[None, :] + 1, 0), axis=1) - 1
    left_over = jnp.sum((~fits).astype(jnp.int32))

    where = jnp.stack([z, x]).astype(jnp.int32)

    def finish(parts):
        x_up, x_down, z_up, z_down = parts[:4]
        got_xu, got_xd = lax.ppermute(x_up, "inner", along_x[1]), lax.ppermute(x_down, "inner", along_x[3])
        got_zu, got_zd = lax.ppermute(z_up, "inner", along_z[1]), lax.ppermute(z_down, "inner", along_z[3])

        def onward(near_up, near_down, got_up, got_down):
            up = jnp.concatenate([near_up[:2] + got_up, near_up[2:]], axis=0)
            down = jnp.concatenate([near_down[:2], near_down[2:] + got_down], axis=0)
            return up, down

        x_up, x_down = onward(parts[4], parts[5], got_xu, got_xd)
        z_up, z_down = onward(parts[7], parts[8], got_zu, got_zd)
        got_xu, got_xd = lax.ppermute(x_up, "inner", along_x[1]), lax.ppermute(x_down, "inner", along_x[3])
        got_zu, got_zd = lax.ppermute(z_up, "inner", along_z[1]), lax.ppermute(z_down, "inner", along_z[3])
        s1 = [parts[6][q] + got_xu[q] + got_xd[q] for q in range(4)]
        s2 = [parts[9][q] + got_zu[q] + got_zd[q] for q in range(4)]
        f1 = [lax.ppermute(s1[s], "inner", along_z[s]) for s in (1, 3, 2)]
        f2 = [lax.ppermute(s2[s], "inner", along_x[s]) for s in (1, 3, 2)]
        return [s1[0] + f1[0] + f1[1] + f1[2], s2[0] + f2[0] + f2[1] + f2[2]]

    p1, p3 = pack(integrals, index, ((1, 0, EARLY), (3, 0, EARLY)), total)
    r1, r3 = lax.ppermute(p1, "grp", along_y[1]), lax.ppermute(p3, "grp", along_y[3])
    codes, _ = lax.optimization_barrier((codes, p1))
    later, _ = lax.optimization_barrier((index, codes))
    p5, p6, p2, p4, p0 = pack(integrals, later, ((1, EARLY, total), (3, EARLY, total), (2, 0, FIRST), (2, FIRST, total), (0, 0, total)), total)
    r5, r6 = lax.ppermute(p5, "grp", along_y[1]), lax.ppermute(p6, "grp", along_y[3])
    r2, r4 = lax.ppermute(p2, "grp", along_y[2]), lax.ppermute(p4, "grp", along_y[2])
    note = jnp.concatenate(
        [
            jnp.broadcast_to(codes.reshape(n_grp, 1, total), (n_grp, n_inner, total)),
            jnp.broadcast_to(left_over, (n_grp, n_inner, 1)),
        ],
        axis=2,
    ).astype(jnp.float32)
    note = lax.all_to_all(note.reshape(devices, total + 1), AXES, split_axis=0, concat_axis=0, tiled=True)
    overflow = jnp.sum(note[:, total]) > 0.5
    note = note[:, :total].reshape(n_grp, n_inner // 2, 2, total)
    note = lax.dynamic_index_in_dim(note, inner // 2, axis=1, keepdims=False)
    note = jnp.stack([lax.dynamic_index_in_dim(note, (grp - s + n_grp) % n_grp, axis=0, keepdims=False) for s in range(4)])
    note = jnp.stack([lax.dynamic_index_in_dim(note, core, axis=1, keepdims=False), lax.dynamic_index_in_dim(note, 1 - core, axis=1, keepdims=False)])
    note = note.astype(jnp.int32)

    def codes_of(*pieces):
        return jnp.concatenate([note[side, s, lo:hi] for side in range(2) for s, lo, hi in pieces])

    def with_other(tiles):
        return [*tiles, *[lax.ppermute(t, "inner", across) for t in tiles]]

    amp = arrange(where, amp)
    acc, token = ladder(codes_of((0, 0, total), (1, 0, EARLY), (3, 0, EARLY), (1, EARLY, total), (3, EARLY, total)), amp, None, with_other([p0, gate(r1, note), gate(r3, note), r5, r6]), False, blocks)
    acc, token = ladder(codes_of((2, 0, FIRST)), amp, acc, with_other([gate(r2, token)]), False, blocks)
    parts = ladder(codes_of((2, FIRST, total)), amp, acc, with_other([gate(r4, token)]), True, blocks)
    pieces = finish(parts)
    out = jnp.concatenate(pieces, axis=1)

    def with_rest(out):
        rest = jnp.where(fits[:, None, None], 0.0, integrals)
        return add(out, slow_part(amplitude, rest, tile_owner, tile_row, tile_col))

    return lax.cond(overflow, with_rest, lambda out: out, out)


def solution(mesh):
    placed = (P(AXES, None), P(AXES, None, None), P(AXES, None), P(AXES), P(AXES))
    return jax.shard_map(per_device, mesh=mesh, in_specs=placed, out_specs=P(AXES, None), check_vma=False)
```

```python
import functools

import jax
import jax.numpy as jnp
from jax import lax
from jax.experimental import pallas as pl
from jax.experimental.pallas import tpu as pltpu
from jax.sharding import PartitionSpec as P

TILE = 128
SLOTS = 40
FIRST = 34
EARLY = 28
VMEM = 24 * 1024 * 1024
AXES = ("grp", "inner")


def slow_part(amplitude, integrals, tile_owner, tile_row, tile_col):
    n_grp, n_inner = lax.axis_size("grp"), lax.axis_size("inner")
    devices = n_grp * n_inner
    count, size = integrals.shape[:2]
    blocks = amplitude.shape[1] // size
    per_dev = blocks // n_inner
    capacity = max(2, 2 * count // devices)
    owners = tile_owner[:, 0]
    order = jnp.arange(count, dtype=jnp.int32)
    same = (owners[:, None] == owners[None, :]) & (order[None, :] < order[:, None])
    slot = owners * capacity + jnp.sum(same.astype(jnp.int32), axis=1)
    position = (tile_row * blocks + tile_col).astype(jnp.float32)
    tiles = jnp.zeros((devices * capacity, size, size), jnp.float32).at[slot].set(integrals)
    place = jnp.zeros((devices * capacity,), jnp.float32).at[slot].set(position)
    tiles, place = (
        lax.all_to_all(tiles, AXES, split_axis=0, concat_axis=0, tiled=True),
        lax.all_to_all(place, AXES, split_axis=0, concat_axis=0, tiled=True),
    )
    dense = jnp.zeros((per_dev * blocks, size, size), jnp.float32).at[place.astype(jnp.int32)].add(tiles)
    dense = dense.reshape(per_dev, blocks, size, size).transpose(0, 2, 1, 3).reshape(per_dev * size, blocks * size)
    slab = lax.all_to_all(amplitude, "inner", split_axis=1, concat_axis=0, tiled=True)
    return lax.psum_scatter(
        jnp.dot(slab, dense, precision=lax.Precision.HIGHEST, preferred_element_type=jnp.float32),
        "inner",
        scatter_dimension=0,
        tiled=True,
    )


def pack_kernel(spans, total, index, tiles, *refs):
    outs, sems = refs[: len(spans)], refs[-1]
    for at, (which, lo, hi) in enumerate(spans):

        def issue(k, _):
            pltpu.make_async_copy(tiles.at[index[which * total + lo + k]], outs[at].at[k], sems.at[at]).start()
            return 0

        lax.fori_loop(0, hi - lo, issue, 0)
    for at, (_, lo, hi) in enumerate(spans):
        pltpu.make_async_copy(tiles.at[pl.ds(0, hi - lo)], outs[at], sems.at[at]).wait()


def pack(integrals, index, spans, total):
    return pl.pallas_call(
        functools.partial(pack_kernel, spans, total),
        out_shape=[jax.ShapeDtypeStruct((hi - lo, TILE, TILE), jnp.float32) for _, lo, hi in spans],
        in_specs=[pl.BlockSpec(memory_space=pltpu.SMEM), pl.BlockSpec(memory_space=pl.ANY)],
        out_specs=[pl.BlockSpec(memory_space=pltpu.VMEM)] * len(spans),
        scratch_shapes=[pltpu.SemaphoreType.DMA((len(spans),))],
        compiler_params=pltpu.CompilerParams(vmem_limit_bytes=16 * 2**20),
        cost_estimate=pl.CostEstimate(flops=0, bytes_accessed=1000, transcendentals=0),
    )(index, integrals)


def add_kernel(one, two, out):
    out[...] = one[...] + two[...]


def add(one, two):
    return pl.pallas_call(add_kernel, out_shape=jax.ShapeDtypeStruct(one.shape, one.dtype))(one, two)


def gate_kernel(*refs):
    pass


def gate(value, *after):
    any_spec = pl.BlockSpec(memory_space=pl.ANY)
    return pl.pallas_call(
        gate_kernel,
        out_shape=jax.ShapeDtypeStruct(value.shape, value.dtype),
        in_specs=[any_spec] * (1 + len(after)),
        out_specs=any_spec,
        input_output_aliases={0: 0},
        compiler_params=pltpu.CompilerParams(vmem_limit_bytes=2**17),
    )(value, *after)


def split(value):
    high = value.astype(jnp.bfloat16)
    return high, (value - high.astype(jnp.float32)).astype(jnp.bfloat16)


def arrange_kernel(where, amp, out, sem):
    z, x = where[0], where[1]
    for sx in range(4):
        for sz in range(4):
            source = lax.rem(z + sz, 4) * 4 + lax.rem(x + sx, 4)
            pltpu.make_async_copy(amp.at[source], out.at[sx * 4 + sz], sem).start()
    pltpu.make_async_copy(amp, out, sem).wait()


def arrange(where, amp):
    return pl.pallas_call(
        arrange_kernel,
        out_shape=pltpu.VMEM(amp.shape, amp.dtype),
        in_specs=[pl.BlockSpec(memory_space=pltpu.SMEM), pl.BlockSpec(memory_space=pl.ANY)],
        out_specs=pl.BlockSpec(memory_space=pltpu.VMEM),
        scratch_shapes=[pltpu.SemaphoreType.DMA],
        compiler_params=pltpu.CompilerParams(vmem_limit_bytes=2**20),
        cost_estimate=pl.CostEstimate(flops=0, bytes_accessed=1000, transcendentals=0),
    )(where, amp)


def ladder_kernel(counts, blocks, first, last, *refs):
    refs, lists = list(refs), len(counts)
    code, amp_v = refs[:2]
    del refs[:2]
    acc_v = None if first else refs.pop(0)
    tiles = refs[:lists]
    del refs[:lists]
    if last:
        parts = [refs.pop(0) for _ in range(10)]
    else:
        acc_v = refs.pop(0)
        token = refs.pop(0)
        token[...] = jnp.zeros_like(token)
    tile_v = refs[:lists]
    tile_sem, out_sem = refs[lists:]

    copies = [pltpu.make_async_copy(tiles[k], tile_v[k], tile_sem.at[k]) for k in range(lists)]
    for copy in copies:
        copy.start()
    if first:
        acc_v[...] = jnp.zeros_like(acc_v)

    for k in range(lists):
        copies[k].wait()
        base = sum(counts[:k])

        def pair(j, _):
            places = [code[base + 2 * j], code[base + 2 * j + 1]]

            @pl.when(jnp.maximum(*places) >= 0)
            def _():
                terms = []
                for half, place in enumerate(places):
                    held = jnp.maximum(place, 0)
                    row = pl.multiple_of((held // blocks) * TILE, TILE)
                    col = pl.multiple_of(lax.rem(held, blocks) * TILE, TILE)
                    a_hi, a_lo = split(amp_v[:, :, pl.ds(row, TILE)].reshape(16 * 8, TILE))
                    t_hi, t_lo = split(jnp.where(place >= 0, tile_v[k][2 * j + half], 0.0))
                    left = jnp.concatenate([a_hi, a_lo], axis=1)
                    right = jnp.concatenate([t_hi, t_lo], axis=1)
                    both = jnp.dot(left, jnp.concatenate([right, right], axis=0), preferred_element_type=jnp.float32)
                    terms.append((col, (both[:, :TILE] + both[:, TILE:]).reshape(4, 4, 8, TILE)))
                for col, term in terms:
                    acc_v[:, :, :, pl.ds(col, TILE)] += term

            return 0

        lax.fori_loop(0, counts[k] // 2, pair, 0)

    if last:
        half = blocks * TILE // 2
        one, two = pl.ds(0, half), pl.ds(half, half)
        sources = [acc_v.at[2, pl.ds(0, 2), :, one], acc_v.at[2, pl.ds(2, 2), :, one]]
        sources += [acc_v.at[pl.ds(0, 2), 2, :, two], acc_v.at[pl.ds(2, 2), 2, :, two]]
        sources += [acc_v.at[s, :, :, one] for s in (1, 3, 0)] + [acc_v.at[:, s, :, two] for s in (1, 3, 0)]
        done = [pltpu.make_async_copy(source, part, out_sem.at[i]) for i, (source, part) in enumerate(zip(sources, parts))]
        for copy in done:
            copy.start()
        for copy in done:
            copy.wait()


def keep(value):
    return pltpu.with_memory_space_constraint(value, pltpu.VMEM)


def ladder(code, amp, acc, tiles, last, blocks):
    counts = tuple(t.shape[0] for t in tiles)
    any_spec, smem, vmem = [pl.BlockSpec(memory_space=m) for m in (pl.ANY, pltpu.SMEM, pltpu.VMEM)]
    held = [] if acc is None else [acc]
    if last:
        shapes = [pltpu.HBM((n, 8, blocks * TILE // 2), jnp.float32) for n in (2,) * 4 + (4,) * 6]
    else:
        shapes = [pltpu.VMEM((4, 4, 8, blocks * TILE), jnp.float32), jax.ShapeDtypeStruct((8, TILE), jnp.float32)]
    return pl.pallas_call(
        functools.partial(ladder_kernel, counts, blocks, acc is None, last),
        out_shape=shapes,
        in_specs=[smem, vmem] + [vmem] * len(held) + [any_spec] * len(tiles),
        out_specs=[any_spec] * len(shapes) if last else [vmem, vmem],
        scratch_shapes=[
            *[pltpu.VMEM((n, TILE, TILE), jnp.float32) for n in counts],
            pltpu.SemaphoreType.DMA((len(tiles),)),
            pltpu.SemaphoreType.DMA((10,)),
        ],
        input_output_aliases={2: 0} if held and not last else {},
        compiler_params=pltpu.CompilerParams(vmem_limit_bytes=VMEM),
        cost_estimate=pl.CostEstimate(flops=0, bytes_accessed=1000, transcendentals=0),
    )(code, keep(amp), *[keep(h) for h in held], *tiles)


def per_device(amplitude, integrals, tile_owner, tile_row, tile_col):
    n_grp, n_inner = lax.axis_size("grp"), lax.axis_size("inner")
    devices = n_grp * n_inner
    rows, width = amplitude.shape
    count = integrals.shape[0]
    blocks = width // TILE
    per_dev = blocks // n_inner
    total = SLOTS
    grp, inner = lax.axis_index("grp"), lax.axis_index("inner")
    z, x, core = inner // 8, (inner // 2) % 4, inner % 2

    def at(z, x, core):
        return (z % 4) * 8 + (x % 4) * 2 + core

    every = [(a, b, c) for a in range(4) for b in range(4) for c in range(2)]
    along_x = {s: [(at(a, b, c), at(a, b + s, c)) for a, b, c in every] for s in (1, 2, 3)}
    along_z = {s: [(at(a, b, c), at(a + s, b, c)) for a, b, c in every] for s in (1, 2, 3)}
    along_y = {s: [(i, (i + s) % n_grp) for i in range(n_grp)] for s in (1, 2, 3)}
    across = [(i, i ^ 1) for i in range(n_inner)]
    same_core = [[at(a, b, c) for a in range(4) for b in range(4)] for c in range(2)]

    amp = lax.all_gather(amplitude, "inner", axis=0, axis_index_groups=same_core)

    owners = tile_owner[:, 0]
    slab = owners // n_inner
    step = (slab - grp + n_grp) % n_grp
    order = jnp.arange(count, dtype=jnp.int32)
    key = tile_col * count + order
    ahead = (slab[:, None] == slab[None, :]) & (key[None, :] < key[:, None])
    rank = jnp.sum(ahead.astype(jnp.int32), axis=1)
    fits = rank < total
    code = ((owners % n_inner) * per_dev + tile_row) * blocks + tile_col
    slots = jnp.arange(n_grp * total, dtype=jnp.int32)[:, None]
    mine = jnp.where(fits, step * total + rank, -1)[None, :] == slots
    index = jnp.sum(jnp.where(mine, order[None, :], 0), axis=1)
    theirs = jnp.where(fits, slab * total + rank, -1)[None, :] == slots
    codes = jnp.sum(jnp.where(theirs, code[None, :] + 1, 0), axis=1) - 1
    left_over = jnp.sum((~fits).astype(jnp.int32))

    where = jnp.stack([z, x]).astype(jnp.int32)

    def finish(parts):
        x_up, x_down, z_up, z_down = parts[:4]
        got_xu, got_xd = lax.ppermute(x_up, "inner", along_x[1]), lax.ppermute(x_down, "inner", along_x[3])
        got_zu, got_zd = lax.ppermute(z_up, "inner", along_z[1]), lax.ppermute(z_down, "inner", along_z[3])

        def onward(near_up, near_down, got_up, got_down):
            up = jnp.concatenate([near_up[:2] + got_up, near_up[2:]], axis=0)
            down = jnp.concatenate([near_down[:2], near_down[2:] + got_down], axis=0)
            return up, down

        x_up, x_down = onward(parts[4], parts[5], got_xu, got_xd)
        z_up, z_down = onward(parts[7], parts[8], got_zu, got_zd)
        got_xu, got_xd = lax.ppermute(x_up, "inner", along_x[1]), lax.ppermute(x_down, "inner", along_x[3])
        got_zu, got_zd = lax.ppermute(z_up, "inner", along_z[1]), lax.ppermute(z_down, "inner", along_z[3])
        s1 = [parts[6][q] + got_xu[q] + got_xd[q] for q in range(4)]
        s2 = [parts[9][q] + got_zu[q] + got_zd[q] for q in range(4)]
        f1 = [lax.ppermute(s1[s], "inner", along_z[s]) for s in (1, 3, 2)]
        f2 = [lax.ppermute(s2[s], "inner", along_x[s]) for s in (1, 3, 2)]
        return [s1[0] + f1[0] + f1[1] + f1[2], s2[0] + f2[0] + f2[1] + f2[2]]

    p1, p3 = pack(integrals, index, ((1, 0, EARLY), (3, 0, EARLY)), total)
    r1, r3 = lax.ppermute(p1, "grp", along_y[1]), lax.ppermute(p3, "grp", along_y[3])
    codes, _ = lax.optimization_barrier((codes, p1))
    later, _ = lax.optimization_barrier((index, codes))
    p5, p6, p2, p4, p0 = pack(integrals, later, ((1, EARLY, total), (3, EARLY, total), (2, 0, FIRST), (2, FIRST, total), (0, 0, total)), total)
    r5, r6 = lax.ppermute(p5, "grp", along_y[1]), lax.ppermute(p6, "grp", along_y[3])
    r2, r4 = lax.ppermute(gate(p2, r5, r6), "grp", along_y[2]), lax.ppermute(p4, "grp", along_y[2])
    note = jnp.concatenate(
        [
            jnp.broadcast_to(codes.reshape(n_grp, 1, total), (n_grp, n_inner, total)),
            jnp.broadcast_to(left_over, (n_grp, n_inner, 1)),
        ],
        axis=2,
    ).astype(jnp.float32)
    note = lax.all_to_all(note.reshape(devices, total + 1), AXES, split_axis=0, concat_axis=0, tiled=True)
    overflow = jnp.sum(note[:, total]) > 0.5
    note = note[:, :total].reshape(n_grp, n_inner // 2, 2, total)
    note = lax.dynamic_index_in_dim(note, inner // 2, axis=1, keepdims=False)
    note = jnp.stack([lax.dynamic_index_in_dim(note, (grp - s + n_grp) % n_grp, axis=0, keepdims=False) for s in range(4)])
    note = jnp.stack([lax.dynamic_index_in_dim(note, core, axis=1, keepdims=False), lax.dynamic_index_in_dim(note, 1 - core, axis=1, keepdims=False)])
    note = note.astype(jnp.int32)

    def codes_of(*pieces):
        return jnp.concatenate([note[side, s, lo:hi] for side in range(2) for s, lo, hi in pieces])

    def with_other(tiles):
        return [*tiles, *[lax.ppermute(t, "inner", across) for t in tiles]]

    amp = arrange(where, amp)
    acc, token = ladder(codes_of((0, 0, total), (1, 0, EARLY), (3, 0, EARLY), (1, EARLY, total), (3, EARLY, total)), amp, None, with_other([p0, gate(r1, note), gate(r3, note), r5, r6]), False, blocks)
    acc, token = ladder(codes_of((2, 0, FIRST)), amp, acc, with_other([gate(r2, token)]), False, blocks)
    parts = ladder(codes_of((2, FIRST, total)), amp, acc, with_other([gate(r4, token)]), True, blocks)
    pieces = finish(parts)
    out = jnp.concatenate(pieces, axis=1)

    def with_rest(out):
        rest = jnp.where(fits[:, None, None], 0.0, integrals)
        return add(out, slow_part(amplitude, rest, tile_owner, tile_row, tile_col))

    return lax.cond(overflow, with_rest, lambda out: out, out)


def solution(mesh):
    placed = (P(AXES, None), P(AXES, None, None), P(AXES, None), P(AXES), P(AXES))
    return jax.shard_map(per_device, mesh=mesh, in_specs=placed, out_specs=P(AXES, None), check_vma=False)
```

```python
import functools

import jax
import jax.numpy as jnp
from jax import lax
from jax.experimental import pallas as pl
from jax.experimental.pallas import tpu as pltpu
from jax.sharding import PartitionSpec as P

TILE = 128
SLOTS = 40
FIRST = 34
EARLY = 28
VMEM = 24 * 1024 * 1024
AXES = ("grp", "inner")


def slow_part(amplitude, integrals, tile_owner, tile_row, tile_col):
    n_grp, n_inner = lax.axis_size("grp"), lax.axis_size("inner")
    devices = n_grp * n_inner
    count, size = integrals.shape[:2]
    blocks = amplitude.shape[1] // size
    per_dev = blocks // n_inner
    capacity = max(2, 2 * count // devices)
    owners = tile_owner[:, 0]
    order = jnp.arange(count, dtype=jnp.int32)
    same = (owners[:, None] == owners[None, :]) & (order[None, :] < order[:, None])
    slot = owners * capacity + jnp.sum(same.astype(jnp.int32), axis=1)
    position = (tile_row * blocks + tile_col).astype(jnp.float32)
    tiles = jnp.zeros((devices * capacity, size, size), jnp.float32).at[slot].set(integrals)
    place = jnp.zeros((devices * capacity,), jnp.float32).at[slot].set(position)
    tiles, place = (
        lax.all_to_all(tiles, AXES, split_axis=0, concat_axis=0, tiled=True),
        lax.all_to_all(place, AXES, split_axis=0, concat_axis=0, tiled=True),
    )
    dense = jnp.zeros((per_dev * blocks, size, size), jnp.float32).at[place.astype(jnp.int32)].add(tiles)
    dense = dense.reshape(per_dev, blocks, size, size).transpose(0, 2, 1, 3).reshape(per_dev * size, blocks * size)
    slab = lax.all_to_all(amplitude, "inner", split_axis=1, concat_axis=0, tiled=True)
    return lax.psum_scatter(
        jnp.dot(slab, dense, precision=lax.Precision.HIGHEST, preferred_element_type=jnp.float32),
        "inner",
        scatter_dimension=0,
        tiled=True,
    )


def pack_kernel(spans, total, index, tiles, *refs):
    outs, sems = refs[: len(spans)], refs[-1]
    for at, (which, lo, hi) in enumerate(spans):

        def issue(k, _):
            pltpu.make_async_copy(tiles.at[index[which * total + lo + k]], outs[at].at[k], sems.at[at]).start()
            return 0

        lax.fori_loop(0, hi - lo, issue, 0)
    for at, (_, lo, hi) in enumerate(spans):
        pltpu.make_async_copy(tiles.at[pl.ds(0, hi - lo)], outs[at], sems.at[at]).wait()


def pack(integrals, index, spans, total):
    return pl.pallas_call(
        functools.partial(pack_kernel, spans, total),
        out_shape=[jax.ShapeDtypeStruct((hi - lo, TILE, TILE), jnp.float32) for _, lo, hi in spans],
        in_specs=[pl.BlockSpec(memory_space=pltpu.SMEM), pl.BlockSpec(memory_space=pl.ANY)],
        out_specs=[pl.BlockSpec(memory_space=pltpu.VMEM)] * len(spans),
        scratch_shapes=[pltpu.SemaphoreType.DMA((len(spans),))],
        compiler_params=pltpu.CompilerParams(vmem_limit_bytes=16 * 2**20),
        cost_estimate=pl.CostEstimate(flops=0, bytes_accessed=1000, transcendentals=0),
    )(index, integrals)


def add_kernel(one, two, out):
    out[...] = one[...] + two[...]


def add(one, two):
    return pl.pallas_call(add_kernel, out_shape=jax.ShapeDtypeStruct(one.shape, one.dtype))(one, two)


def gate_kernel(*refs):
    pass


def gate(value, *after, array=jax.ShapeDtypeStruct):
    any_spec = pl.BlockSpec(memory_space=pl.ANY)
    return pl.pallas_call(
        gate_kernel,
        out_shape=array(value.shape, value.dtype),
        in_specs=[any_spec] * (1 + len(after)),
        out_specs=any_spec,
        input_output_aliases={0: 0},
        compiler_params=pltpu.CompilerParams(vmem_limit_bytes=2**17),
    )(value, *after)


def split(value):
    high = value.astype(jnp.bfloat16)
    return high, (value - high.astype(jnp.float32)).astype(jnp.bfloat16)


def arrange_kernel(where, amp, out, sem):
    z, x = where[0], where[1]
    for sx in range(4):
        for sz in range(4):
            source = lax.rem(z + sz, 4) * 4 + lax.rem(x + sx, 4)
            pltpu.make_async_copy(amp.at[source], out.at[sx * 4 + sz], sem).start()
    pltpu.make_async_copy(amp, out, sem).wait()


def arrange(where, amp):
    return pl.pallas_call(
        arrange_kernel,
        out_shape=pltpu.VMEM(amp.shape, amp.dtype),
        in_specs=[pl.BlockSpec(memory_space=pltpu.SMEM), pl.BlockSpec(memory_space=pl.ANY)],
        out_specs=pl.BlockSpec(memory_space=pltpu.VMEM),
        scratch_shapes=[pltpu.SemaphoreType.DMA],
        compiler_params=pltpu.CompilerParams(vmem_limit_bytes=2**20),
        cost_estimate=pl.CostEstimate(flops=0, bytes_accessed=1000, transcendentals=0),
    )(where, amp)


def ladder_kernel(counts, blocks, first, last, *refs):
    refs, lists = list(refs), len(counts)
    code, amp_v = refs[:2]
    del refs[:2]
    acc_v = None if first else refs.pop(0)
    tiles = refs[:lists]
    del refs[:lists]
    if last:
        parts = [refs.pop(0) for _ in range(10)]
    else:
        acc_v = refs.pop(0)
        token = refs.pop(0)
        token[...] = jnp.zeros_like(token)
    tile_v = refs[:lists]
    tile_sem, out_sem = refs[lists:]

    copies = [pltpu.make_async_copy(tiles[k], tile_v[k], tile_sem.at[k]) for k in range(lists)]
    for copy in copies:
        copy.start()
    if first:
        acc_v[...] = jnp.zeros_like(acc_v)

    for k in range(lists):
        copies[k].wait()
        base = sum(counts[:k])

        def pair(j, _):
            places = [code[base + 2 * j], code[base + 2 * j + 1]]

            @pl.when(jnp.maximum(*places) >= 0)
            def _():
                terms = []
                for half, place in enumerate(places):
                    held = jnp.maximum(place, 0)
                    row = pl.multiple_of((held // blocks) * TILE, TILE)
                    col = pl.multiple_of(lax.rem(held, blocks) * TILE, TILE)
                    a_hi, a_lo = split(amp_v[:, :, pl.ds(row, TILE)].reshape(16 * 8, TILE))
                    t_hi, t_lo = split(jnp.where(place >= 0, tile_v[k][2 * j + half], 0.0))
                    left = jnp.concatenate([a_hi, a_lo], axis=1)
                    right = jnp.concatenate([t_hi, t_lo], axis=1)
                    both = jnp.dot(left, jnp.concatenate([right, right], axis=0), preferred_element_type=jnp.float32)
                    terms.append((col, (both[:, :TILE] + both[:, TILE:]).reshape(4, 4, 8, TILE)))
                for col, term in terms:
                    acc_v[:, :, :, pl.ds(col, TILE)] += term

            return 0

        lax.fori_loop(0, counts[k] // 2, pair, 0)

    if last:
        half = blocks * TILE // 2
        one, two = pl.ds(0, half), pl.ds(half, half)
        sources = [acc_v.at[2, pl.ds(0, 2), :, one], acc_v.at[2, pl.ds(2, 2), :, one]]
        sources += [acc_v.at[pl.ds(0, 2), 2, :, two], acc_v.at[pl.ds(2, 2), 2, :, two]]
        sources += [acc_v.at[s, :, :, one] for s in (1, 3, 0)] + [acc_v.at[:, s, :, two] for s in (1, 3, 0)]
        done = [pltpu.make_async_copy(source, part, out_sem.at[i]) for i, (source, part) in enumerate(zip(sources, parts))]
        for copy in done:
            copy.start()
        for copy in done:
            copy.wait()


def keep(value):
    return pltpu.with_memory_space_constraint(value, pltpu.VMEM)


def ladder(code, amp, acc, tiles, last, blocks):
    counts = tuple(t.shape[0] for t in tiles)
    any_spec, smem, vmem = [pl.BlockSpec(memory_space=m) for m in (pl.ANY, pltpu.SMEM, pltpu.VMEM)]
    held = [] if acc is None else [acc]
    if last:
        shapes = [pltpu.HBM((n, 8, blocks * TILE // 2), jnp.float32) for n in (2,) * 4 + (4,) * 6]
    else:
        shapes = [pltpu.VMEM((4, 4, 8, blocks * TILE), jnp.float32), jax.ShapeDtypeStruct((8, TILE), jnp.float32)]
    return pl.pallas_call(
        functools.partial(ladder_kernel, counts, blocks, acc is None, last),
        out_shape=shapes,
        in_specs=[smem, vmem] + [vmem] * len(held) + [any_spec] * len(tiles),
        out_specs=[any_spec] * len(shapes) if last else [vmem, vmem],
        scratch_shapes=[
            *[pltpu.VMEM((n, TILE, TILE), jnp.float32) for n in counts],
            pltpu.SemaphoreType.DMA((len(tiles),)),
            pltpu.SemaphoreType.DMA((10,)),
        ],
        input_output_aliases={2: 0} if held and not last else {},
        compiler_params=pltpu.CompilerParams(vmem_limit_bytes=VMEM),
        cost_estimate=pl.CostEstimate(flops=0, bytes_accessed=1000, transcendentals=0),
    )(code, keep(amp), *[keep(h) for h in held], *tiles)


def per_device(amplitude, integrals, tile_owner, tile_row, tile_col):
    n_grp, n_inner = lax.axis_size("grp"), lax.axis_size("inner")
    devices = n_grp * n_inner
    rows, width = amplitude.shape
    count = integrals.shape[0]
    blocks = width // TILE
    per_dev = blocks // n_inner
    total = SLOTS
    grp, inner = lax.axis_index("grp"), lax.axis_index("inner")
    z, x, core = inner // 8, (inner // 2) % 4, inner % 2

    def at(z, x, core):
        return (z % 4) * 8 + (x % 4) * 2 + core

    every = [(a, b, c) for a in range(4) for b in range(4) for c in range(2)]
    along_x = {s: [(at(a, b, c), at(a, b + s, c)) for a, b, c in every] for s in (1, 2, 3)}
    along_z = {s: [(at(a, b, c), at(a + s, b, c)) for a, b, c in every] for s in (1, 2, 3)}
    along_y = {s: [(i, (i + s) % n_grp) for i in range(n_grp)] for s in (1, 2, 3)}
    across = [(i, i ^ 1) for i in range(n_inner)]
    same_core = [[at(a, b, c) for a in range(4) for b in range(4)] for c in range(2)]

    amp = lax.all_gather(amplitude, "inner", axis=0, axis_index_groups=same_core)

    owners = tile_owner[:, 0]
    slab = owners // n_inner
    step = (slab - grp + n_grp) % n_grp
    order = jnp.arange(count, dtype=jnp.int32)
    key = tile_col * count + order
    ahead = (slab[:, None] == slab[None, :]) & (key[None, :] < key[:, None])
    rank = jnp.sum(ahead.astype(jnp.int32), axis=1)
    fits = rank < total
    code = ((owners % n_inner) * per_dev + tile_row) * blocks + tile_col
    slots = jnp.arange(n_grp * total, dtype=jnp.int32)[:, None]
    mine = jnp.where(fits, step * total + rank, -1)[None, :] == slots
    index = jnp.sum(jnp.where(mine, order[None, :], 0), axis=1)
    theirs = jnp.where(fits, slab * total + rank, -1)[None, :] == slots
    codes = jnp.sum(jnp.where(theirs, code[None, :] + 1, 0), axis=1) - 1
    left_over = jnp.sum((~fits).astype(jnp.int32))

    where = jnp.stack([z, x]).astype(jnp.int32)

    def finish(parts):
        x_up, x_down, z_up, z_down = parts[:4]
        got_xu, got_xd = lax.ppermute(x_up, "inner", along_x[1]), lax.ppermute(x_down, "inner", along_x[3])
        got_zu, got_zd = lax.ppermute(z_up, "inner", along_z[1]), lax.ppermute(z_down, "inner", along_z[3])

        def onward(near_up, near_down, got_up, got_down):
            up = jnp.concatenate([near_up[:2] + got_up, near_up[2:]], axis=0)
            down = jnp.concatenate([near_down[:2], near_down[2:] + got_down], axis=0)
            return up, down

        x_up, x_down = onward(parts[4], parts[5], got_xu, got_xd)
        z_up, z_down = onward(parts[7], parts[8], got_zu, got_zd)
        got_xu, got_xd = lax.ppermute(x_up, "inner", along_x[1]), lax.ppermute(x_down, "inner", along_x[3])
        got_zu, got_zd = lax.ppermute(z_up, "inner", along_z[1]), lax.ppermute(z_down, "inner", along_z[3])
        s1 = [parts[6][q] + got_xu[q] + got_xd[q] for q in range(4)]
        s2 = [parts[9][q] + got_zu[q] + got_zd[q] for q in range(4)]
        f1 = [lax.ppermute(s1[s], "inner", along_z[s]) for s in (1, 3, 2)]
        f2 = [lax.ppermute(s2[s], "inner", along_x[s]) for s in (1, 3, 2)]
        return [s1[0] + f1[0] + f1[1] + f1[2], s2[0] + f2[0] + f2[1] + f2[2]]

    p1, p3 = pack(integrals, index, ((1, 0, EARLY), (3, 0, EARLY)), total)
    r1, r3 = lax.ppermute(p1, "grp", along_y[1]), lax.ppermute(p3, "grp", along_y[3])
    codes, _ = lax.optimization_barrier((codes, p1))
    later, _ = lax.optimization_barrier((index, codes))
    p5, p6, p2, p4, p0 = pack(integrals, later, ((1, EARLY, total), (3, EARLY, total), (2, 0, FIRST), (2, FIRST, total), (0, 0, total)), total)
    r5, r6 = lax.ppermute(p5, "grp", along_y[1]), lax.ppermute(p6, "grp", along_y[3])
    r2, r4 = lax.ppermute(gate(pltpu.with_memory_space_constraint(p2, pltpu.HBM), r5, r6, array=pltpu.HBM), "grp", along_y[2]), lax.ppermute(p4, "grp", along_y[2])
    note = jnp.concatenate(
        [
            jnp.broadcast_to(codes.reshape(n_grp, 1, total), (n_grp, n_inner, total)),
            jnp.broadcast_to(left_over, (n_grp, n_inner, 1)),
        ],
        axis=2,
    ).astype(jnp.float32)
    note = lax.all_to_all(note.reshape(devices, total + 1), AXES, split_axis=0, concat_axis=0, tiled=True)
    overflow = jnp.sum(note[:, total]) > 0.5
    note = note[:, :total].reshape(n_grp, n_inner // 2, 2, total)
    note = lax.dynamic_index_in_dim(note, inner // 2, axis=1, keepdims=False)
    note = jnp.stack([lax.dynamic_index_in_dim(note, (grp - s + n_grp) % n_grp, axis=0, keepdims=False) for s in range(4)])
    note = jnp.stack([lax.dynamic_index_in_dim(note, core, axis=1, keepdims=False), lax.dynamic_index_in_dim(note, 1 - core, axis=1, keepdims=False)])
    note = note.astype(jnp.int32)

    def codes_of(*pieces):
        return jnp.concatenate([note[side, s, lo:hi] for side in range(2) for s, lo, hi in pieces])

    def with_other(tiles):
        return [*tiles, *[lax.ppermute(t, "inner", across) for t in tiles]]

    amp = arrange(where, amp)
    acc, token = ladder(codes_of((0, 0, total), (1, 0, EARLY), (3, 0, EARLY), (1, EARLY, total), (3, EARLY, total)), amp, None, with_other([p0, gate(r1, note), gate(r3, note), r5, r6]), False, blocks)
    token, overflow = lax.optimization_barrier((token, overflow))
    acc, token = ladder(codes_of((2, 0, FIRST)), amp, acc, with_other([gate(r2, token)]), False, blocks)
    parts = ladder(codes_of((2, FIRST, total)), amp, acc, with_other([gate(r4, token)]), True, blocks)
    pieces = finish(parts)
    out = jnp.concatenate(pieces, axis=1)

    def with_rest(out):
        rest = jnp.where(fits[:, None, None], 0.0, integrals)
        return add(out, slow_part(amplitude, rest, tile_owner, tile_row, tile_col))

    return lax.cond(overflow, with_rest, lambda out: out, out)


def solution(mesh):
    placed = (P(AXES, None), P(AXES, None, None), P(AXES, None), P(AXES), P(AXES))
    return jax.shard_map(per_device, mesh=mesh, in_specs=placed, out_specs=P(AXES, None), check_vma=False)
```

```python
import functools

import jax
import jax.numpy as jnp
from jax import lax
from jax.experimental import pallas as pl
from jax.experimental.pallas import tpu as pltpu
from jax.sharding import PartitionSpec as P

TILE = 128
SLOTS = 40
FIRST = 32
EARLY = 28
VMEM = 24 * 1024 * 1024
AXES = ("grp", "inner")


def slow_part(amplitude, integrals, tile_owner, tile_row, tile_col):
    n_grp, n_inner = lax.axis_size("grp"), lax.axis_size("inner")
    devices = n_grp * n_inner
    count, size = integrals.shape[:2]
    blocks = amplitude.shape[1] // size
    per_dev = blocks // n_inner
    capacity = max(2, 2 * count // devices)
    owners = tile_owner[:, 0]
    order = jnp.arange(count, dtype=jnp.int32)
    same = (owners[:, None] == owners[None, :]) & (order[None, :] < order[:, None])
    slot = owners * capacity + jnp.sum(same.astype(jnp.int32), axis=1)
    position = (tile_row * blocks + tile_col).astype(jnp.float32)
    tiles = jnp.zeros((devices * capacity, size, size), jnp.float32).at[slot].set(integrals)
    place = jnp.zeros((devices * capacity,), jnp.float32).at[slot].set(position)
    tiles, place = (
        lax.all_to_all(tiles, AXES, split_axis=0, concat_axis=0, tiled=True),
        lax.all_to_all(place, AXES, split_axis=0, concat_axis=0, tiled=True),
    )
    dense = jnp.zeros((per_dev * blocks, size, size), jnp.float32).at[place.astype(jnp.int32)].add(tiles)
    dense = dense.reshape(per_dev, blocks, size, size).transpose(0, 2, 1, 3).reshape(per_dev * size, blocks * size)
    slab = lax.all_to_all(amplitude, "inner", split_axis=1, concat_axis=0, tiled=True)
    return lax.psum_scatter(
        jnp.dot(slab, dense, precision=lax.Precision.HIGHEST, preferred_element_type=jnp.float32),
        "inner",
        scatter_dimension=0,
        tiled=True,
    )


def pack_kernel(spans, total, index, tiles, *refs):
    outs, sems = refs[: len(spans)], refs[-1]
    for at, (which, lo, hi) in enumerate(spans):

        def issue(k, _):
            pltpu.make_async_copy(tiles.at[index[which * total + lo + k]], outs[at].at[k], sems.at[at]).start()
            return 0

        lax.fori_loop(0, hi - lo, issue, 0)
    for at, (_, lo, hi) in enumerate(spans):
        pltpu.make_async_copy(tiles.at[pl.ds(0, hi - lo)], outs[at], sems.at[at]).wait()


def pack(integrals, index, spans, total):
    return pl.pallas_call(
        functools.partial(pack_kernel, spans, total),
        out_shape=[jax.ShapeDtypeStruct((hi - lo, TILE, TILE), jnp.float32) for _, lo, hi in spans],
        in_specs=[pl.BlockSpec(memory_space=pltpu.SMEM), pl.BlockSpec(memory_space=pl.ANY)],
        out_specs=[pl.BlockSpec(memory_space=pltpu.VMEM)] * len(spans),
        scratch_shapes=[pltpu.SemaphoreType.DMA((len(spans),))],
        compiler_params=pltpu.CompilerParams(vmem_limit_bytes=16 * 2**20),
        cost_estimate=pl.CostEstimate(flops=0, bytes_accessed=1000, transcendentals=0),
    )(index, integrals)


def add_kernel(one, two, out):
    out[...] = one[...] + two[...]


def add(one, two):
    return pl.pallas_call(add_kernel, out_shape=jax.ShapeDtypeStruct(one.shape, one.dtype))(one, two)


def gate_kernel(*refs):
    pass


def gate(value, *after, array=jax.ShapeDtypeStruct):
    any_spec = pl.BlockSpec(memory_space=pl.ANY)
    return pl.pallas_call(
        gate_kernel,
        out_shape=array(value.shape, value.dtype),
        in_specs=[any_spec] * (1 + len(after)),
        out_specs=any_spec,
        input_output_aliases={0: 0},
        compiler_params=pltpu.CompilerParams(vmem_limit_bytes=2**17),
    )(value, *after)


def split(value):
    high = value.astype(jnp.bfloat16)
    return high, (value - high.astype(jnp.float32)).astype(jnp.bfloat16)


def arrange_kernel(where, amp, out, sem):
    z, x = where[0], where[1]
    for sx in range(4):
        for sz in range(4):
            source = lax.rem(z + sz, 4) * 4 + lax.rem(x + sx, 4)
            pltpu.make_async_copy(amp.at[source], out.at[sx * 4 + sz], sem).start()
    pltpu.make_async_copy(amp, out, sem).wait()


def arrange(where, amp):
    return pl.pallas_call(
        arrange_kernel,
        out_shape=pltpu.VMEM(amp.shape, amp.dtype),
        in_specs=[pl.BlockSpec(memory_space=pltpu.SMEM), pl.BlockSpec(memory_space=pl.ANY)],
        out_specs=pl.BlockSpec(memory_space=pltpu.VMEM),
        scratch_shapes=[pltpu.SemaphoreType.DMA],
        compiler_params=pltpu.CompilerParams(vmem_limit_bytes=2**20),
        cost_estimate=pl.CostEstimate(flops=0, bytes_accessed=1000, transcendentals=0),
    )(where, amp)


def ladder_kernel(counts, blocks, first, last, *refs):
    refs, lists = list(refs), len(counts)
    code, amp_v = refs[:2]
    del refs[:2]
    acc_v = None if first else refs.pop(0)
    tiles = refs[:lists]
    del refs[:lists]
    if last:
        parts = [refs.pop(0) for _ in range(10)]
    else:
        acc_v = refs.pop(0)
        token = refs.pop(0)
        token[...] = jnp.zeros_like(token)
    tile_v = refs[:lists]
    tile_sem, out_sem = refs[lists:]

    copies = [pltpu.make_async_copy(tiles[k], tile_v[k], tile_sem.at[k]) for k in range(lists)]
    for copy in copies:
        copy.start()
    if first:
        acc_v[...] = jnp.zeros_like(acc_v)

    for k in range(lists):
        copies[k].wait()
        base = sum(counts[:k])
        group = 4 if counts[k] % 4 == 0 else 2

        def pair(j, _):
            places = [code[base + group * j + i] for i in range(group)]

            @pl.when(functools.reduce(jnp.maximum, places) >= 0)
            def _():
                terms = []
                for half, place in enumerate(places):
                    held = jnp.maximum(place, 0)
                    row = pl.multiple_of((held // blocks) * TILE, TILE)
                    col = pl.multiple_of(lax.rem(held, blocks) * TILE, TILE)
                    a_hi, a_lo = split(amp_v[:, :, pl.ds(row, TILE)].reshape(16 * 8, TILE))
                    t_hi, t_lo = split(jnp.where(place >= 0, tile_v[k][group * j + half], 0.0))
                    left = jnp.concatenate([a_hi, a_lo], axis=1)
                    right = jnp.concatenate([t_hi, t_lo], axis=1)
                    both = jnp.dot(left, jnp.concatenate([right, right], axis=0), preferred_element_type=jnp.float32)
                    terms.append((col, (both[:, :TILE] + both[:, TILE:]).reshape(4, 4, 8, TILE)))
                for col, term in terms:
                    acc_v[:, :, :, pl.ds(col, TILE)] += term

            return 0

        lax.fori_loop(0, counts[k] // group, pair, 0)

    if last:
        half = blocks * TILE // 2
        one, two = pl.ds(0, half), pl.ds(half, half)
        sources = [acc_v.at[2, pl.ds(0, 2), :, one], acc_v.at[2, pl.ds(2, 2), :, one]]
        sources += [acc_v.at[pl.ds(0, 2), 2, :, two], acc_v.at[pl.ds(2, 2), 2, :, two]]
        sources += [acc_v.at[s, :, :, one] for s in (1, 3, 0)] + [acc_v.at[:, s, :, two] for s in (1, 3, 0)]
        done = [pltpu.make_async_copy(source, part, out_sem.at[i]) for i, (source, part) in enumerate(zip(sources, parts))]
        for copy in done:
            copy.start()
        for copy in done:
            copy.wait()


def keep(value):
    return pltpu.with_memory_space_constraint(value, pltpu.VMEM)


def ladder(code, amp, acc, tiles, last, blocks):
    counts = tuple(t.shape[0] for t in tiles)
    any_spec, smem, vmem = [pl.BlockSpec(memory_space=m) for m in (pl.ANY, pltpu.SMEM, pltpu.VMEM)]
    held = [] if acc is None else [acc]
    if last:
        shapes = [pltpu.HBM((n, 8, blocks * TILE // 2), jnp.float32) for n in (2,) * 4 + (4,) * 6]
    else:
        shapes = [pltpu.VMEM((4, 4, 8, blocks * TILE), jnp.float32), jax.ShapeDtypeStruct((8, TILE), jnp.float32)]
    return pl.pallas_call(
        functools.partial(ladder_kernel, counts, blocks, acc is None, last),
        out_shape=shapes,
        in_specs=[smem, vmem] + [vmem] * len(held) + [any_spec] * len(tiles),
        out_specs=[any_spec] * len(shapes) if last else [vmem, vmem],
        scratch_shapes=[
            *[pltpu.VMEM((n, TILE, TILE), jnp.float32) for n in counts],
            pltpu.SemaphoreType.DMA((len(tiles),)),
            pltpu.SemaphoreType.DMA((10,)),
        ],
        input_output_aliases={2: 0} if held and not last else {},
        compiler_params=pltpu.CompilerParams(vmem_limit_bytes=VMEM),
        cost_estimate=pl.CostEstimate(flops=0, bytes_accessed=1000, transcendentals=0),
    )(code, keep(amp), *[keep(h) for h in held], *tiles)


def per_device(amplitude, integrals, tile_owner, tile_row, tile_col):
    n_grp, n_inner = lax.axis_size("grp"), lax.axis_size("inner")
    devices = n_grp * n_inner
    rows, width = amplitude.shape
    count = integrals.shape[0]
    blocks = width // TILE
    per_dev = blocks // n_inner
    total = SLOTS
    grp, inner = lax.axis_index("grp"), lax.axis_index("inner")
    z, x, core = inner // 8, (inner // 2) % 4, inner % 2

    def at(z, x, core):
        return (z % 4) * 8 + (x % 4) * 2 + core

    every = [(a, b, c) for a in range(4) for b in range(4) for c in range(2)]
    along_x = {s: [(at(a, b, c), at(a, b + s, c)) for a, b, c in every] for s in (1, 2, 3)}
    along_z = {s: [(at(a, b, c), at(a + s, b, c)) for a, b, c in every] for s in (1, 2, 3)}
    along_y = {s: [(i, (i + s) % n_grp) for i in range(n_grp)] for s in (1, 2, 3)}
    across = [(i, i ^ 1) for i in range(n_inner)]
    same_core = [[at(a, b, c) for a in range(4) for b in range(4)] for c in range(2)]

    amp = lax.all_gather(amplitude, "inner", axis=0, axis_index_groups=same_core)

    owners = tile_owner[:, 0]
    slab = owners // n_inner
    step = (slab - grp + n_grp) % n_grp
    order = jnp.arange(count, dtype=jnp.int32)
    key = tile_col * count + order
    ahead = (slab[:, None] == slab[None, :]) & (key[None, :] < key[:, None])
    rank = jnp.sum(ahead.astype(jnp.int32), axis=1)
    fits = rank < total
    code = ((owners % n_inner) * per_dev + tile_row) * blocks + tile_col
    slots = jnp.arange(n_grp * total, dtype=jnp.int32)[:, None]
    mine = jnp.where(fits, step * total + rank, -1)[None, :] == slots
    index = jnp.sum(jnp.where(mine, order[None, :], 0), axis=1)
    theirs = jnp.where(fits, slab * total + rank, -1)[None, :] == slots
    codes = jnp.sum(jnp.where(theirs, code[None, :] + 1, 0), axis=1) - 1
    left_over = jnp.sum((~fits).astype(jnp.int32))

    where = jnp.stack([z, x]).astype(jnp.int32)

    def finish(parts):
        x_up, x_down, z_up, z_down = parts[:4]
        got_xu, got_xd = lax.ppermute(x_up, "inner", along_x[1]), lax.ppermute(x_down, "inner", along_x[3])
        got_zu, got_zd = lax.ppermute(z_up, "inner", along_z[1]), lax.ppermute(z_down, "inner", along_z[3])

        def onward(near_up, near_down, got_up, got_down):
            up = jnp.concatenate([near_up[:2] + got_up, near_up[2:]], axis=0)
            down = jnp.concatenate([near_down[:2], near_down[2:] + got_down], axis=0)
            return up, down

        x_up, x_down = onward(parts[4], parts[5], got_xu, got_xd)
        z_up, z_down = onward(parts[7], parts[8], got_zu, got_zd)
        got_xu, got_xd = lax.ppermute(x_up, "inner", along_x[1]), lax.ppermute(x_down, "inner", along_x[3])
        got_zu, got_zd = lax.ppermute(z_up, "inner", along_z[1]), lax.ppermute(z_down, "inner", along_z[3])
        s1 = [parts[6][q] + got_xu[q] + got_xd[q] for q in range(4)]
        s2 = [parts[9][q] + got_zu[q] + got_zd[q] for q in range(4)]
        f1 = [lax.ppermute(s1[s], "inner", along_z[s]) for s in (1, 3, 2)]
        f2 = [lax.ppermute(s2[s], "inner", along_x[s]) for s in (1, 3, 2)]
        return [s1[0] + f1[0] + f1[1] + f1[2], s2[0] + f2[0] + f2[1] + f2[2]]

    p1, p3 = pack(integrals, index, ((1, 0, EARLY), (3, 0, EARLY)), total)
    r1, r3 = lax.ppermute(p1, "grp", along_y[1]), lax.ppermute(p3, "grp", along_y[3])
    codes, _ = lax.optimization_barrier((codes, p1))
    later, _ = lax.optimization_barrier((index, codes))
    p5, p6, p2, p4, p0 = pack(integrals, later, ((1, EARLY, total), (3, EARLY, total), (2, 0, FIRST), (2, FIRST, total), (0, 0, total)), total)
    r5, r6 = lax.ppermute(p5, "grp", along_y[1]), lax.ppermute(p6, "grp", along_y[3])
    r2, r4 = lax.ppermute(gate(pltpu.with_memory_space_constraint(p2, pltpu.HBM), r5, r6, array=pltpu.HBM), "grp", along_y[2]), lax.ppermute(p4, "grp", along_y[2])
    note = jnp.concatenate(
        [
            jnp.broadcast_to(codes.reshape(n_grp, 1, total), (n_grp, n_inner, total)),
            jnp.broadcast_to(left_over, (n_grp, n_inner, 1)),
        ],
        axis=2,
    ).astype(jnp.float32)
    note = lax.all_to_all(note.reshape(devices, total + 1), AXES, split_axis=0, concat_axis=0, tiled=True)
    overflow = jnp.sum(note[:, total]) > 0.5
    note = note[:, :total].reshape(n_grp, n_inner // 2, 2, total)
    note = lax.dynamic_index_in_dim(note, inner // 2, axis=1, keepdims=False)
    note = jnp.stack([lax.dynamic_index_in_dim(note, (grp - s + n_grp) % n_grp, axis=0, keepdims=False) for s in range(4)])
    note = jnp.stack([lax.dynamic_index_in_dim(note, core, axis=1, keepdims=False), lax.dynamic_index_in_dim(note, 1 - core, axis=1, keepdims=False)])
    note = note.astype(jnp.int32)

    def codes_of(*pieces):
        return jnp.concatenate([note[side, s, lo:hi] for side in range(2) for s, lo, hi in pieces])

    def with_other(tiles):
        return [*tiles, *[lax.ppermute(t, "inner", across) for t in tiles]]

    amp = arrange(where, amp)
    acc, token = ladder(codes_of((0, 0, total), (1, 0, EARLY), (3, 0, EARLY), (1, EARLY, total), (3, EARLY, total)), amp, None, with_other([p0, gate(r1, note), gate(r3, note), r5, r6]), False, blocks)
    token, overflow = lax.optimization_barrier((token, overflow))
    acc, token = ladder(codes_of((2, 0, FIRST)), amp, acc, with_other([gate(r2, token)]), False, blocks)
    parts = ladder(codes_of((2, FIRST, total)), amp, acc, with_other([gate(r4, token)]), True, blocks)
    pieces = finish(parts)
    out = jnp.concatenate(pieces, axis=1)

    def with_rest(out):
        rest = jnp.where(fits[:, None, None], 0.0, integrals)
        return add(out, slow_part(amplitude, rest, tile_owner, tile_row, tile_col))

    return lax.cond(overflow, with_rest, lambda out: out, out)


def solution(mesh):
    placed = (P(AXES, None), P(AXES, None, None), P(AXES, None), P(AXES), P(AXES))
    return jax.shard_map(per_device, mesh=mesh, in_specs=placed, out_specs=P(AXES, None), check_vma=False)
```
